32 devices in a mesh: tm: 16 (over z, y, core), space: 2 (over x).
Axes of the slice: x: 2, y: 2, z: 4, core: 2. Of those that a mesh axis runs over, the one named last changes fastest.
Arguments:
- start_state: float32 [16, 64, 2048], P('tm', None, 'space'), may hold values from -1.2 to 1.2
- stiffness: float32 [64, 64], replicated, may hold values from -0.75 to 0.75
- lifting: float32 [64, 96], replicated, may hold values from -0.625 to 0.625
- coarse: float32 [64, 64], replicated
- neighbor: int32 [6, 2048], P(None, 'space'), may hold values from 0 to 2047, as said below
- orientation: int32 [6, 2048], P(None, 'space'), may hold values from 0 to 7
- send_low: int32 [1024], P('space'), may hold values from 0 to 1023, as said below
- send_high: int32 [1024], P('space'), may hold values from 0 to 1023, as said below
Outputs:
- end_state: float32 [16, 64, 2048], P('tm', None, 'space')
The draws below stay inside these ranges and needn't reach their ends.
Inputs may be any that keep to these rules, and one draw needn't show every extreme that they name: `send_low`: distinct local slots of one partition, 512 per partition; the lower boundary elements of a partition are the upper neighbours, across face 1, of the upper boundary elements of the partition below, in the same order. `send_high`: distinct local slots of one partition, 512 per partition. `neighbor`: values of 1024 or more occur only for face 0 (first 512 halo slots) and face 1 (next 512 halo slots); each halo slot is named by exactly one element.
All inputs are finite; a program needn't handle non-finite values.
Results may differ from the reference program's by a relative error of at most 0.00015.
Values sent between devices are 32-bit elements; how exact they have to be, the bound alone decides.
A program may use at most 64 MiB of HBM per device.

```python
import jax
import jax.numpy as jnp
from jax import lax

NODES = 64
STEPS = 3
CXE = 2
EY = 16
EZ = 32
E_DEV = 1024
BND = 512
NE = 2048
SLICES = 16
N_SPACE = 2


def relabel(orders, device_ids, value, position):
    current = orders[:, position]
    swapped = jnp.where(orders == value, current[:, None], jnp.where(orders == current[:, None], value, orders))
    return jnp.where(device_ids[:, None], swapped, orders).astype(jnp.int32)


def layout(key):
    base_key = jax.random.fold_in(key, 11)
    orders = jax.vmap(lambda device_id: jax.random.permutation(jax.random.fold_in(base_key, device_id), E_DEV))(jnp.arange(N_SPACE))
    orders = orders.astype(jnp.int32)
    device_ids = jnp.arange(N_SPACE, dtype=jnp.int32)
    first_dev = device_ids == 0
    last_dev = device_ids == N_SPACE - 1
    orders = relabel(orders, first_dev, E_DEV - 1, 0)
    orders = relabel(orders, first_dev, 0, E_DEV - 1)
    orders = relabel(orders, last_dev, E_DEV - 1, E_DEV - 1)
    orders = relabel(orders, last_dev, 0, 0)
    cell_ids = jnp.arange(E_DEV, dtype=jnp.int32)
    plane = EY * EZ
    slab_layer = cell_ids // plane
    plane_row = cell_ids // EZ % EY
    plane_col = cell_ids % EZ
    bnd_index = plane_row * EZ + plane_col

    def cell_at(layer_id, row_id, col_id):
        return layer_id * plane + row_id * EZ + col_id
    face_low = jnp.where(slab_layer[None, :] > 0, orders[:, cell_at(jnp.maximum(slab_layer - 1, 0), plane_row, plane_col)], E_DEV + bnd_index[None, :])
    face_high = jnp.where(slab_layer[None, :] < CXE - 1, orders[:, cell_at(jnp.minimum(slab_layer + 1, CXE - 1), plane_row, plane_col)], E_DEV + BND + bnd_index[None, :])
    face_two = orders[:, cell_at(slab_layer, (plane_row - 1) % EY, plane_col)]
    face_three = orders[:, cell_at(slab_layer, (plane_row + 1) % EY, plane_col)]
    face_four = orders[:, cell_at(slab_layer, plane_row, (plane_col - 1) % EZ)]
    face_five = orders[:, cell_at(slab_layer, plane_row, (plane_col + 1) % EZ)]
    values = jnp.stack([face_low, face_high, face_two, face_three, face_four, face_five]).astype(jnp.int32)
    placed = jnp.zeros((6, N_SPACE, E_DEV), jnp.int32).at[:, jnp.arange(N_SPACE)[:, None], orders].set(values)
    return (placed.reshape(6, N_SPACE * E_DEV), orders[:, :BND].reshape(-1), orders[:, (CXE - 1) * BND:].reshape(-1))


def draw_neighbor(key, part):
    return layout(key)[0]


def draw_send_low(key, part):
    return layout(key)[1]


def draw_send_high(key, part):
    return layout(key)[2]


def draw_coarse(key, part):
    diag_key = jax.random.fold_in(key, 21)
    off_key = jax.random.fold_in(key, 22)
    diag_vals = jnp.exp(jax.random.uniform(diag_key, (NODES,), jnp.float32, jnp.log(0.6), jnp.log(0.85)))
    off_vals = 0.02 * jax.random.normal(off_key, (NODES, NODES), jnp.float32)
    identity = jnp.eye(NODES, dtype=jnp.float32)
    return off_vals * (1.0 - identity) + identity * diag_vals[None, :]


def set_ends(result, own_key, low, top_value):
    extent = result.shape
    place = [jax.random.randint(jax.random.fold_in(own_key, axis), (), 0, extent[axis]) for axis in range(len(extent))]
    result = result.at[tuple(place)].set(low)
    longest = extent.index(max(extent))
    place[longest] = (place[longest] + 1) % extent[longest]
    return result.at[tuple(place)].set(top_value)


def steps_of(own_key, shape, shards, low, largest):
    loudness, own = 1.0, jax.random.fold_in(own_key, 6)
    for axis_at, parts in shards:
        heights = jnp.exp(jax.random.uniform(jax.random.fold_in(own, axis_at), (parts,), jnp.float32, low / len(shards), largest / len(shards)))
        loudness = loudness * jnp.repeat(heights, shape[axis_at] // parts).reshape([-1 if axis == axis_at else 1 for axis in range(len(shape))])
    return loudness


def bell_draw(own_key, shape, scale, bound, kind=jnp.bfloat16):
    array = jax.random.normal(own_key, shape, jnp.float32) * scale
    return jnp.minimum(jnp.maximum(array, -bound), bound).astype(kind)


def setup_inputs(seed: int = 0) -> dict:
    splits = jax.random.split(jax.random.key(seed), 9)
    return {
        "start_state": jnp.clip(jax.random.uniform(splits[0], (SLICES, NODES, NE), jnp.float32, -1.2, 1.2) * steps_of(splits[0], (SLICES, NODES, NE), ((0, 16), (2, 2)), -0.4, 0.0), -1.2, 1.2),
        "stiffness": bell_draw(splits[1], (NODES, NODES), NODES ** -0.5, 0.75, jnp.float32),
        "lifting": bell_draw(splits[2], (NODES, 6 * 16), (6 * 16) ** -0.5, 0.625, jnp.float32),
        "coarse": draw_coarse(jax.random.fold_in(splits[8], 71), 0),
        "neighbor": draw_neighbor(jax.random.fold_in(splits[8], 71), 0),
        "orientation": set_ends(jax.random.randint(splits[5], (6, NE), 0, 8), jax.random.fold_in(splits[5], 1), 0, 7).astype(jnp.int32),
        "send_low": draw_send_low(jax.random.fold_in(splits[8], 71), 0),
        "send_high": draw_send_high(jax.random.fold_in(splits[8], 71), 0),
    }


time_step = 0.05


def product(matrix, vector):
    return jnp.dot(matrix, vector, precision=lax.Precision.HIGHEST, preferred_element_type=jnp.float32)


def face_traces(state_now):
    elements = state_now.shape[1]
    cube_view = state_now.reshape(4, 4, 4, elements)
    return [cube_view[0], cube_view[3], cube_view[:, 0], cube_view[:, 3], cube_view[:, :, 0], cube_view[:, :, 3]]


def oriented(trace, code_row):
    summed = jnp.zeros_like(trace)
    for variant in range(8):
        turned = trace
        if variant & 4:
            turned = jnp.swapaxes(turned, 0, 1)
        if variant & 1:
            turned = turned[::-1]
        if variant & 2:
            turned = turned[:, ::-1]
        summed = summed + jnp.where(code_row == variant, turned, 0.0)
    return summed


def tendency(state_now, own_list, near_list, stiffness, lifting, orientation):
    elements = state_now.shape[1]
    jump_list = []
    for face_id in range(6):
        jump_list.append((oriented(near_list[face_id], orientation[face_id]) - own_list[face_id]).reshape(16, elements))
    stacked = jnp.concatenate(jump_list, axis=0)
    return product(stiffness, state_now) + product(lifting, stacked) + state_now - state_now * state_now * state_now


def reference(start_state, stiffness, lifting, coarse, neighbor, orientation, send_low, send_high):
    total = E_DEV * N_SPACE
    device_of = jnp.arange(total, dtype=jnp.int32) // E_DEV
    lower_dev = (device_of - 1) % N_SPACE
    upper_dev = (device_of + 1) % N_SPACE
    low_index = jnp.clip(neighbor - E_DEV, 0, BND - 1).astype(jnp.int32)
    high_index = jnp.clip(neighbor - E_DEV - BND, 0, BND - 1).astype(jnp.int32)
    from_lower = lower_dev * E_DEV + send_high[lower_dev * BND + low_index]
    from_upper = upper_dev * E_DEV + send_low[upper_dev * BND + high_index]
    global_nb = jnp.where(neighbor < E_DEV, device_of * E_DEV + neighbor,
                          jnp.where(neighbor < E_DEV + BND, from_lower, from_upper)).astype(jnp.int32)

    def fine_slice(state_now):
        for step_id in range(STEPS):
            own_list = face_traces(state_now)
            near_list = []
            for face_id in range(6):
                source = own_list[face_id ^ 1].reshape(16, total)
                near_list.append(jnp.take(source, global_nb[face_id], axis=1).reshape(4, 4, total))
            state_now = state_now + time_step * tendency(state_now, own_list, near_list, stiffness, lifting, orientation)
        return state_now

    fine_all = lax.map(fine_slice, start_state)
    defect = fine_all - jax.vmap(lambda slice_state: product(coarse, slice_state))(start_state)

    def advance(carry_state, defect_now):
        end_now = product(coarse, carry_state) + defect_now
        return end_now, end_now

    last_state, ends = lax.scan(advance, start_state[0], defect)
    return ends
```

```python
import functools

import jax
import jax.numpy as jnp
from jax import lax
from jax.experimental import pallas as pl
from jax.experimental.pallas import tpu as pltpu
from jax.sharding import PartitionSpec as P

STEPS = 3
GROUP = 4
LANES = 128
WIDE = 256
MESH = pl.DeviceIdType.MESH

time_step = 0.05


def exact(a, b):
    return jnp.dot(a, b, precision=lax.Precision.HIGHEST, preferred_element_type=jnp.float32)


def parts_of(value):
    head = value.astype(jnp.bfloat16)
    tail = (value - head.astype(jnp.float32)).astype(jnp.bfloat16)
    return head, tail


def keep_split(ref, value):
    rows = value.shape[0]
    head, tail = parts_of(value)
    ref[0:rows, :] = head
    ref[rows : 2 * rows, :] = tail


def split_dot(ref, value):
    rows = ref.shape[0] // 2
    head, tail = parts_of(value)
    both = jnp.dot(ref[...], head, preferred_element_type=jnp.float32)
    rest = jnp.dot(ref[0:rows, :], tail, preferred_element_type=jnp.float32)
    return both[:rows] + (both[rows:] + rest)


def along(value, index, axis):
    return jnp.take_along_axis(value, index, axis=axis, mode="promise_in_bounds")


def pick(sources, index):
    lane = index & (LANES - 1)
    tile = index >> 7
    upper = lower = None
    for number, load in sources:
        first, second = load()
        first, second = along(first, lane, 1), along(second, lane, 1)
        if upper is None:
            upper, lower = first, second
        else:
            here = tile == number
            upper, lower = jnp.where(here, first, upper), jnp.where(here, second, lower)
    return upper, lower


def selection():
    row = lax.broadcasted_iota(jnp.int32, (96, 64), 0)
    node = lax.broadcasted_iota(jnp.int32, (96, 64), 1)
    face, a, b = row >> 4, (row >> 2) & 3, row & 3
    place = jnp.where(
        face < 2, 4 * a + b, jnp.where(face < 4, 16 * a + b, 16 * a + 4 * b)
    ) + jnp.where(face == 1, 48, jnp.where(face == 3, 12, jnp.where(face == 5, 3, 0)))
    return jnp.where(place == node, 1.0, 0.0).astype(jnp.float32)


def kernel(
    n_time, n_space,
    start_ref, stiff_ref, lift_ref, coarse_ref, near_ref, turn_ref, low_ref, high_ref,
    out_ref,
    stack, trace, spot, coarse_start, leave, halo, joined, weights, reach, powers, last_power, one_power,
    defect, gathered, prefix, carry, ends, final,
    halo_send, halo_recv, mix_send, mix_recv, chain_send, chain_recv, back_send, back_recv,
):
    elements = start_ref.shape[2]
    tiles = elements // LANES
    bound = low_ref.shape[1]
    bound_tiles = bound // LANES
    quarter = elements // GROUP
    me_t, me_s = lax.axis_index("tm"), lax.axis_index("space")
    group, rank = me_t // GROUP, me_t % GROUP
    first = group * GROUP
    groups = n_time // GROUP
    below, above = (me_s + n_space - 1) % n_space, (me_s + 1) % n_space
    mates = [first + (rank + by) % GROUP for by in range(1, GROUP)]
    following = (me_t + GROUP) % n_time
    previous = (me_t + n_time - GROUP) % n_time

    barrier = pltpu.get_barrier_semaphore()
    for space in (below, above):
        pl.semaphore_signal(barrier, inc=1, device_id=(me_t, space), device_id_type=MESH)
    for time in mates + [following, previous]:
        pl.semaphore_signal(barrier, inc=1, device_id=(time, me_s), device_id_type=MESH)

    def keep_traces(tile):
        for i in range(4):
            trace[tile, 0, 4 * i : 4 * i + 4, :] = stack[tile, 16 * i : 16 * i + 4, :]
            trace[tile, 1, 4 * i : 4 * i + 4, :] = stack[tile, 16 * i + 12 : 16 * i + 16, :]
        trace[tile, 2] = stack[tile, pl.ds(0, 16, stride=4), :]
        trace[tile, 3] = stack[tile, pl.ds(3, 16, stride=4), :]

    for tile in range(tiles):
        stack[tile, 0:64, :] = start_ref[0, :, tile * LANES : (tile + 1) * LANES]

    def local_source(face, s):
        if face == 0:
            return s, lambda: (stack[s, 0:8, :], stack[s, 8:16, :])
        if face == 1:
            return s, lambda: (stack[s, 48:56, :], stack[s, 56:64, :])
        return s, lambda: (trace[s, face - 2, 0:8, :], trace[s, face - 2, 8:16, :])

    def wide_index(ref, row, t):
        at = pl.multiple_of(t * LANES, LANES)
        return jnp.broadcast_to(ref[row : row + 1, pl.ds(at, LANES)], (8, LANES))

    def halo_copies(step):
        return [
            pltpu.make_async_remote_copy(
                src_ref=leave.at[step, side],
                dst_ref=halo.at[step, side],
                send_sem=halo_send.at[step, side],
                recv_sem=halo_recv.at[step, side],
                device_id=(me_t, target),
                device_id_type=MESH,
            )
            for side, target in ((0, below), (1, above))
        ]

    def send_halo(step):
        def fill(t, _):
            for side, ref in ((0, low_ref), (1, high_ref)):
                sources = [local_source(side, s) for s in range(tiles)]
                upper, lower = pick(sources, wide_index(ref, 0, t))
                leave[step, side, t, 0:8, :] = upper
                leave[step, side, t, 8:16, :] = lower
            return 0

        lax.fori_loop(0, bound_tiles, fill, 0)
        if step == 0:
            pl.semaphore_wait(barrier, 2 + GROUP - 1 + 2)
        copies = halo_copies(step)
        for copy in copies:
            copy.start()
        return copies

    def place(face, t, upper, lower):
        for half in range(2):
            index = spot[face, t, 8 * half : 8 * half + 8, :]
            row = index & 7
            turned = jnp.where(index < 8, along(upper, row, 0), along(lower, row, 0))
            at = 64 + 16 * face + 8 * half
            stack[t, at : at + 8, :] = turned

    def inner_faces(t, _):
        for face in range(2, 6):
            sources = [local_source(face ^ 1, s) for s in range(tiles)]
            place(face, t, *pick(sources, wide_index(near_ref, face, t)))
        return 0

    def outer_faces(step):
        def body(t, _):
            for face in range(2):
                side = 1 - face
                sources = [local_source(face ^ 1, s) for s in range(tiles)]
                for b in range(bound_tiles):
                    number = tiles + face * bound_tiles + b
                    sources.append(
                        (
                            number,
                            lambda b=b: (
                                halo[step, side, b, 0:8, :],
                                halo[step, side, b, 8:16, :],
                            ),
                        )
                    )
                place(face, t, *pick(sources, wide_index(near_ref, face, t)))
            return 0

        return body

    copies = send_halo(0)

    def spots(t, _):
        row = lax.broadcasted_iota(jnp.int32, (16, LANES), 0)
        at = pl.multiple_of(t * LANES, LANES)
        for face in range(6):
            code = jnp.broadcast_to(turn_ref[face : face + 1, pl.ds(at, LANES)], (16, LANES))
            a, b = row >> 2, row & 3
            a = jnp.where((code & 1) != 0, 3 - a, a)
            b = jnp.where((code & 2) != 0, 3 - b, b)
            spot[face, t] = jnp.where((code & 4) != 0, 4 * b + a, 4 * a + b)
        return 0

    lax.fori_loop(0, tiles, spots, 0)
    for tile in range(tiles):
        keep_traces(tile)
    lifting = lift_ref[...]
    row64 = lax.broadcasted_iota(jnp.int32, (64, 64), 0)
    col64 = lax.broadcasted_iota(jnp.int32, (64, 64), 1)
    unit = jnp.where(row64 == col64, 1.0, 0.0).astype(jnp.float32)
    joined[:, 0:64] = stiff_ref[...] - exact(lifting, selection()) + unit
    joined[:, 64:160] = lifting
    keep_split(weights, joined[...])
    one = coarse_ref[...]
    two = exact(one, one)
    three = exact(two, one)
    four = exact(two, two)
    keep_split(one_power, one)
    keep_split(last_power, four)
    for part in range(2):
        for at, power in enumerate((one, two, three)):
            value = parts_of(power)[part]
            powers[192 * part + 64 * at : 192 * part + 64 * at + 64, :] = value
    zero = jnp.zeros((64, 64), jnp.float32)
    table = ((one, zero, zero), (two, one, zero), (three, two, one))
    for i in range(3):
        line = jnp.concatenate(table[i], axis=1)
        head, tail = parts_of(line)
        reach[64 * i : 64 * i + 64, :] = head
        reach[192 + 64 * i : 256 + 64 * i, :] = tail
    for c in range(elements // WIDE):
        columns = start_ref[0, :, c * WIDE : (c + 1) * WIDE]
        coarse_start[c] = jnp.where(me_t == 0, 0.0, split_dot(one_power, columns))

    for step in range(STEPS):
        if step > 0:
            copies = send_halo(step)
            for tile in range(tiles):
                keep_traces(tile)
        lax.fori_loop(0, tiles, inner_faces, 0)
        for copy in copies:
            copy.wait()
        lax.fori_loop(0, tiles, outer_faces(step), 0)
        for c in range(elements // WIDE):
            operand = jnp.concatenate([stack[2 * c], stack[2 * c + 1]], axis=1)
            state = operand[0:64]
            rate = split_dot(weights, operand) - state * state * state
            later = state + time_step * rate
            if step < STEPS - 1:
                stack[2 * c, 0:64, :] = later[:, :LANES]
                stack[2 * c + 1, 0:64, :] = later[:, LANES:]
            else:
                q, at = c * WIDE // quarter, c * WIDE % quarter
                defect[q, :, at : at + WIDE] = later - coarse_start[c]

    def exchange(source, target, send, recv):
        out = []
        for by in range(1, GROUP):
            other = (rank + by) % GROUP
            out.append(
                pltpu.make_async_remote_copy(
                    src_ref=source.at[other],
                    dst_ref=target.at[rank],
                    send_sem=send.at[by - 1],
                    recv_sem=recv.at[by - 1],
                    device_id=(first + other, me_s),
                    device_id_type=MESH,
                )
            )
        for copy in out:
            copy.start()
        target[rank] = source[rank]
        for copy in out:
            copy.wait()

    exchange(defect, gathered, mix_send, mix_recv)
    inputs = jnp.concatenate([gathered[0], gathered[1], gathered[2]], axis=0)
    reached = split_dot(reach, inputs)
    prefix[0] = gathered[0]
    for m in range(1, GROUP):
        prefix[m] = gathered[m] + reached[64 * m - 64 : 64 * m]

    chain = pltpu.make_async_remote_copy(
        src_ref=ends.at[GROUP - 1],
        dst_ref=carry,
        send_sem=chain_send,
        recv_sem=chain_recv,
        device_id=(following, me_s),
        device_id_type=MESH,
    )

    @pl.when(group == 0)
    def _():
        carry[...] = jnp.zeros_like(carry)

    @pl.when(group > 0)
    def _():
        chain.wait_recv()

    ends[GROUP - 1] = prefix[GROUP - 1] + split_dot(last_power, carry[...])

    @pl.when(group < groups - 1)
    def _():
        chain.start()

    spread = split_dot(powers, carry[...])
    for m in range(GROUP - 1):
        ends[m] = prefix[m] + spread[64 * m : 64 * m + 64]
    exchange(ends, final, back_send, back_recv)

    @pl.when(group < groups - 1)
    def _():
        chain.wait_send()

    for q in range(GROUP):
        out_ref[0, :, q * quarter : (q + 1) * quarter] = final[q]


def shards(start_state, stiffness, lifting, coarse, neighbor, orientation, send_low, send_high):
    elements = start_state.shape[2]
    bound = send_low.shape[0]
    tiles, bound_tiles, quarter = elements // LANES, bound // LANES, elements // GROUP
    f32, b16, i32 = jnp.float32, jnp.bfloat16, jnp.int32
    dma = pltpu.SemaphoreType.DMA
    vmem = pl.BlockSpec(memory_space=pltpu.VMEM)
    return pl.pallas_call(
        functools.partial(kernel, lax.axis_size("tm"), lax.axis_size("space")),
        out_shape=jax.ShapeDtypeStruct(start_state.shape, f32),
        in_specs=[vmem] * 8,
        out_specs=vmem,
        scratch_shapes=[
            pltpu.VMEM((tiles, 160, LANES), f32),
            pltpu.VMEM((tiles, 4, 16, LANES), f32),
            pltpu.VMEM((6, tiles, 16, LANES), i32),
            pltpu.VMEM((elements // WIDE, 64, WIDE), f32),
            pltpu.VMEM((STEPS, 2, bound_tiles, 16, LANES), f32),
            pltpu.VMEM((STEPS, 2, bound_tiles, 16, LANES), f32),
            pltpu.VMEM((64, 160), f32),
            pltpu.VMEM((128, 160), b16),
            pltpu.VMEM((384, 192), b16),
            pltpu.VMEM((384, 64), b16),
            pltpu.VMEM((128, 64), b16),
            pltpu.VMEM((128, 64), b16),
            pltpu.VMEM((GROUP, 64, quarter), f32),
            pltpu.VMEM((GROUP, 64, quarter), f32),
            pltpu.VMEM((GROUP, 64, quarter), f32),
            pltpu.VMEM((64, quarter), f32),
            pltpu.VMEM((GROUP, 64, quarter), f32),
            pltpu.VMEM((GROUP, 64, quarter), f32),
            dma((STEPS, 2)),
            dma((STEPS, 2)),
            dma((GROUP - 1,)),
            dma((GROUP - 1,)),
            dma,
            dma,
            dma((GROUP - 1,)),
            dma((GROUP - 1,)),
        ],
        compiler_params=pltpu.CompilerParams(
            collective_id=0, has_side_effects=True, vmem_limit_bytes=40 * 1024 * 1024
        ),
    )(
        start_state, stiffness, lifting, coarse, neighbor, orientation,
        send_low.reshape(1, bound), send_high.reshape(1, bound),
    )


def solution(mesh):
    return jax.shard_map(
        shards,
        mesh=mesh,
        in_specs=(
            P("tm", None, "space"),
            P(),
            P(),
            P(),
            P(None, "space"),
            P(None, "space"),
            P("space"),
            P("space"),
        ),
        out_specs=P("tm", None, "space"),
        check_vma=False,
    )
```

```python
import functools

import jax
import jax.numpy as jnp
from jax import lax
from jax.experimental import pallas as pl
from jax.experimental.pallas import tpu as pltpu
from jax.sharding import PartitionSpec as P

STEPS = 3
GROUP = 4
LANES = 128
WIDE = 256
MESH = pl.DeviceIdType.MESH

time_step = 0.05


def exact(a, b):
    return jnp.dot(a, b, precision=lax.Precision.HIGHEST, preferred_element_type=jnp.float32)


def parts_of(value):
    head = value.astype(jnp.bfloat16)
    tail = (value - head.astype(jnp.float32)).astype(jnp.bfloat16)
    return head, tail


def keep_split(ref, value):
    rows = value.shape[0]
    head, tail = parts_of(value)
    ref[0:rows, :] = head
    ref[rows : 2 * rows, :] = tail


def split_dot(ref, value):
    rows = ref.shape[0] // 2
    head, tail = parts_of(value)
    both = jnp.dot(ref[...], head, preferred_element_type=jnp.float32)
    rest = jnp.dot(ref[0:rows, :], tail, preferred_element_type=jnp.float32)
    return both[:rows] + (both[rows:] + rest)


def along(value, index, axis):
    return jnp.take_along_axis(value, index, axis=axis, mode="promise_in_bounds")


def pick(sources, index):
    lane = index & (LANES - 1)
    tile = index >> 7
    upper = lower = None
    for number, load in sources:
        first, second = load()
        first, second = along(first, lane, 1), along(second, lane, 1)
        if upper is None:
            upper, lower = first, second
        else:
            here = tile == number
            upper, lower = jnp.where(here, first, upper), jnp.where(here, second, lower)
    return upper, lower


def selection():
    row = lax.broadcasted_iota(jnp.int32, (96, 64), 0)
    node = lax.broadcasted_iota(jnp.int32, (96, 64), 1)
    face, a, b = row >> 4, (row >> 2) & 3, row & 3
    place = jnp.where(
        face < 2, 4 * a + b, jnp.where(face < 4, 16 * a + b, 16 * a + 4 * b)
    ) + jnp.where(face == 1, 48, jnp.where(face == 3, 12, jnp.where(face == 5, 3, 0)))
    return jnp.where(place == node, 1.0, 0.0).astype(jnp.float32)


def kernel(
    n_time, n_space,
    start_ref, stiff_ref, lift_ref, coarse_ref, near_ref, turn_ref, low_ref, high_ref,
    out_ref,
    stack, trace, spot, coarse_start, leave, halo, joined, weights, reach, powers, last_power, one_power,
    defect, gathered, carry, ends, final,
    start_in, stiff_in, lift_in, coarse_in, near_in, turn_in, low_in, high_in, load_sem, state_sem,
    halo_send, halo_recv, mix_send, mix_recv, chain_send, chain_recv, back_send, back_recv,
):
    elements = start_ref.shape[2]
    loads = {}
    for number, (name, source, target) in enumerate(
        (
            ("low", low_ref, low_in),
            ("high", high_ref, high_in),
            ("turn", turn_ref, turn_in),
            ("stiff", stiff_ref, stiff_in),
            ("lift", lift_ref, lift_in),
            ("near", near_ref, near_in),
            ("coarse", coarse_ref, coarse_in),
            ("start", start_ref, start_in),
        )
    ):
        loads[name] = pltpu.make_async_copy(source, target, load_sem.at[number])
    for name in ("low", "high"):
        loads[name].start()
    states = []
    for tile in range(elements // LANES):
        states.append(
            pltpu.make_async_copy(
                start_ref.at[0, :, tile * LANES : (tile + 1) * LANES],
                stack.at[tile, 0:64, :],
                state_sem.at[tile],
            )
        )
        states[-1].start()
    for name in ("turn", "stiff", "lift", "near", "coarse", "start"):
        loads[name].start()
    tiles = elements // LANES
    bound = low_ref.shape[1]
    bound_tiles = bound // LANES
    quarter = elements // GROUP
    me_t, me_s = lax.axis_index("tm"), lax.axis_index("space")
    group, rank = me_t // GROUP, me_t % GROUP
    first = group * GROUP
    groups = n_time // GROUP
    below, above = (me_s + n_space - 1) % n_space, (me_s + 1) % n_space
    mates = [first + (rank + by) % GROUP for by in range(1, GROUP)]
    following = (me_t + GROUP) % n_time
    previous = (me_t + n_time - GROUP) % n_time

    barrier = pltpu.get_barrier_semaphore()
    for space in (below, above):
        pl.semaphore_signal(barrier, inc=1, device_id=(me_t, space), device_id_type=MESH)
    for time in mates + [following, previous]:
        pl.semaphore_signal(barrier, inc=1, device_id=(time, me_s), device_id_type=MESH)

    def keep_traces(tile):
        for i in range(4):
            trace[tile, 0, 4 * i : 4 * i + 4, :] = stack[tile, 16 * i : 16 * i + 4, :]
            trace[tile, 1, 4 * i : 4 * i + 4, :] = stack[tile, 16 * i + 12 : 16 * i + 16, :]
        trace[tile, 2] = stack[tile, pl.ds(0, 16, stride=4), :]
        trace[tile, 3] = stack[tile, pl.ds(3, 16, stride=4), :]

    loads["low"].wait()
    loads["high"].wait()
    for copy in states:
        copy.wait()

    def local_source(face, s):
        if face == 0:
            return s, lambda: (stack[s, 0:8, :], stack[s, 8:16, :])
        if face == 1:
            return s, lambda: (stack[s, 48:56, :], stack[s, 56:64, :])
        return s, lambda: (trace[s, face - 2, 0:8, :], trace[s, face - 2, 8:16, :])

    def wide_index(ref, row, t):
        at = pl.multiple_of(t * LANES, LANES)
        return jnp.broadcast_to(ref[row : row + 1, pl.ds(at, LANES)], (8, LANES))

    def halo_copies(step):
        return [
            pltpu.make_async_remote_copy(
                src_ref=leave.at[step, side],
                dst_ref=halo.at[step, side],
                send_sem=halo_send.at[step, side],
                recv_sem=halo_recv.at[step, side],
                device_id=(me_t, target),
                device_id_type=MESH,
            )
            for side, target in ((0, below), (1, above))
        ]

    def send_halo(step):
        def fill(t, _):
            for side, ref in ((0, low_in), (1, high_in)):
                sources = [local_source(side, s) for s in range(tiles)]
                upper, lower = pick(sources, wide_index(ref, 0, t))
                leave[step, side, t, 0:8, :] = upper
                leave[step, side, t, 8:16, :] = lower
            return 0

        lax.fori_loop(0, bound_tiles, fill, 0, unroll=4)
        if step == 0:
            pl.semaphore_wait(barrier, 2 + GROUP - 1 + 2)
        copies = halo_copies(step)
        for copy in copies:
            copy.start()
        return copies

    def place(face, t, upper, lower):
        for half in range(2):
            index = spot[face, t, 8 * half : 8 * half + 8, :]
            row = index & 7
            turned = jnp.where(index < 8, along(upper, row, 0), along(lower, row, 0))
            at = 64 + 16 * face + 8 * half
            stack[t, at : at + 8, :] = turned

    def inner_faces(t, _):
        for face in range(2, 6):
            sources = [local_source(face ^ 1, s) for s in range(tiles)]
            place(face, t, *pick(sources, wide_index(near_in, face, t)))
        return 0

    def outer_faces(step):
        def body(t, _):
            for face in range(2):
                side = 1 - face
                sources = [local_source(face ^ 1, s) for s in range(tiles)]
                for b in range(bound_tiles):
                    number = tiles + face * bound_tiles + b
                    sources.append(
                        (
                            number,
                            lambda b=b: (
                                halo[step, side, b, 0:8, :],
                                halo[step, side, b, 8:16, :],
                            ),
                        )
                    )
                place(face, t, *pick(sources, wide_index(near_in, face, t)))
            return 0

        return body

    copies = send_halo(0)

    def spots(t, _):
        row = lax.broadcasted_iota(jnp.int32, (16, LANES), 0)
        at = pl.multiple_of(t * LANES, LANES)
        for face in range(6):
            code = jnp.broadcast_to(turn_in[face : face + 1, pl.ds(at, LANES)], (16, LANES))
            a, b = row >> 2, row & 3
            a = jnp.where((code & 1) != 0, 3 - a, a)
            b = jnp.where((code & 2) != 0, 3 - b, b)
            spot[face, t] = jnp.where((code & 4) != 0, 4 * b + a, 4 * a + b)
        return 0

    loads["turn"].wait()
    lax.fori_loop(0, tiles, spots, 0)
    for tile in range(tiles):
        keep_traces(tile)

    def fine_matrix():
        loads["stiff"].wait()
        loads["lift"].wait()
        lifting = lift_in[...]
        row64 = lax.broadcasted_iota(jnp.int32, (64, 64), 0)
        col64 = lax.broadcasted_iota(jnp.int32, (64, 64), 1)
        unit = jnp.where(row64 == col64, 1.0, 0.0).astype(jnp.float32)
        joined[:, 0:64] = stiff_in[...] - exact(lifting, selection()) + unit
        joined[:, 64:160] = lifting
        keep_split(weights, joined[...])

    def coarse_matrices():
        loads["coarse"].wait()
        one = coarse_in[...]
        two = exact(one, one)
        three = exact(two, one)
        four = exact(two, two)
        keep_split(one_power, one)
        keep_split(last_power, four)
        for part in range(2):
            for at, power in enumerate((one, two, three)):
                value = parts_of(power)[part]
                powers[192 * part + 64 * at : 192 * part + 64 * at + 64, :] = value
        zero = jnp.zeros((64, 64), jnp.float32)
        table = ((one, zero, zero), (two, one, zero), (three, two, one))
        for i in range(3):
            line = jnp.concatenate(table[i], axis=1)
            head, tail = parts_of(line)
            reach[64 * i : 64 * i + 64, :] = head
            reach[192 + 64 * i : 256 + 64 * i, :] = tail

    def coarse_first():
        loads["start"].wait()
        for c in range(elements // WIDE):
            columns = start_in[0, :, c * WIDE : (c + 1) * WIDE]
            coarse_start[c] = jnp.where(me_t == 0, 0.0, split_dot(one_power, columns))

    def advance(c):
        operand = jnp.concatenate([stack[2 * c], stack[2 * c + 1]], axis=1)
        state = operand[0:64]
        rate = split_dot(weights, operand) - state * state * state
        return state + time_step * rate

    for step in range(STEPS):
        if step > 0:
            copies = send_halo(step)
            for tile in range(tiles):
                keep_traces(tile)
        if step == 0:
            fine_matrix()
            loads["near"].wait()
        lax.fori_loop(0, tiles, inner_faces, 0, unroll=4)
        if step == 1:
            coarse_matrices()
        if step == 2:
            coarse_first()
        for copy in copies:
            copy.wait()
        lax.fori_loop(0, tiles, outer_faces(step), 0, unroll=4)
        if step < STEPS - 1:
            for c in range(elements // WIDE):
                later = advance(c)
                stack[2 * c, 0:64, :] = later[:, :LANES]
                stack[2 * c + 1, 0:64, :] = later[:, LANES:]

    pairs = (None, rank + 1 - 2 * (rank % 2), (rank + 2) % GROUP, GROUP - 1 - rank)

    def swap(source, target, send, recv, by, half):
        other = pairs[by]
        return pltpu.make_async_remote_copy(
            src_ref=source.at[other, half],
            dst_ref=target.at[rank, half],
            send_sem=send.at[by - 1, half],
            recv_sem=recv.at[by - 1, half],
            device_id=(first + other, me_s),
            device_id_type=MESH,
        )

    def last_step(q, target, slot):
        for w in range(quarter // WIDE):
            c = q * (quarter // WIDE) + w
            value = advance(c) - coarse_start[c]
            for piece in range(2):
                at = w * WIDE + piece * LANES
                half, column = at // (quarter // 2), at % (quarter // 2)
                target[slot, half, :, column : column + LANES] = value[
                    :, piece * LANES : (piece + 1) * LANES
                ]

    mixes = {(by, h): swap(defect, gathered, mix_send, mix_recv, by, h) for by in (2, 3, 1) for h in (0, 1)}
    for by in (2, 3, 1):
        last_step(pairs[by], defect, pairs[by])
        mixes[by, 0].start()
    for by in (2, 3, 1):
        mixes[by, 1].start()
    last_step(rank, gathered, rank)

    chain = [
        pltpu.make_async_remote_copy(
            src_ref=ends.at[GROUP - 1, h],
            dst_ref=carry.at[h],
            send_sem=chain_send.at[h],
            recv_sem=chain_recv.at[h],
            device_id=(following, me_s),
            device_id_type=MESH,
        )
        for h in range(2)
    ]
    backs = {(by, h): swap(ends, final, back_send, back_recv, by, h) for by in (2, 3, 1) for h in (0, 1)}

    def give_back(h):
        for by in (2, 3, 1):
            backs[by, h].start()
        final[rank, h] = ends[rank, h]

    for h in range(2):
        for by in (1, 2, 3):
            mixes[by, h].wait_recv()
        inputs = jnp.concatenate([gathered[0, h], gathered[1, h], gathered[2, h]], axis=0)
        reached = split_dot(reach, inputs)
        ends[0, h] = gathered[0, h]
        for m in range(1, GROUP):
            ends[m, h] = gathered[m, h] + reached[64 * m - 64 : 64 * m]

        @pl.when(group == 0)
        def _():
            if groups > 1:
                chain[h].start()
            give_back(h)

    @pl.when(group > 0)
    def _():
        for h in range(2):
            chain[h].wait_recv()
            held = carry[h]
            ends[GROUP - 1, h] = ends[GROUP - 1, h] + split_dot(last_power, held)

            @pl.when(group < groups - 1)
            def _():
                chain[h].start()

            spread = split_dot(powers, held)
            for m in range(GROUP - 1):
                ends[m, h] = ends[m, h] + spread[64 * m : 64 * m + 64]
            give_back(h)

    for copy in mixes.values():
        copy.wait_send()

    @pl.when(group < groups - 1)
    def _():
        for h in range(2):
            chain[h].wait_send()

    for h in range(2):
        for by in (1, 2, 3):
            backs[by, h].wait()
        for q in range(GROUP):
            at = q * quarter + h * (quarter // 2)
            out_ref[0, :, at : at + quarter // 2] = final[q, h]


def shards(start_state, stiffness, lifting, coarse, neighbor, orientation, send_low, send_high):
    elements = start_state.shape[2]
    bound = send_low.shape[0]
    tiles, bound_tiles, quarter = elements // LANES, bound // LANES, elements // GROUP
    f32, b16, i32 = jnp.float32, jnp.bfloat16, jnp.int32
    dma = pltpu.SemaphoreType.DMA
    vmem = pl.BlockSpec(memory_space=pltpu.VMEM)
    return pl.pallas_call(
        functools.partial(kernel, lax.axis_size("tm"), lax.axis_size("space")),
        out_shape=jax.ShapeDtypeStruct(start_state.shape, f32),
        in_specs=[pl.BlockSpec(memory_space=pltpu.HBM)] * 8,
        out_specs=vmem,
        scratch_shapes=[
            pltpu.VMEM((tiles, 160, LANES), f32),
            pltpu.VMEM((tiles, 4, 16, LANES), f32),
            pltpu.VMEM((6, tiles, 16, LANES), i32),
            pltpu.VMEM((elements // WIDE, 64, WIDE), f32),
            pltpu.VMEM((STEPS, 2, bound_tiles, 16, LANES), f32),
            pltpu.VMEM((STEPS, 2, bound_tiles, 16, LANES), f32),
            pltpu.VMEM((64, 160), f32),
            pltpu.VMEM((128, 160), b16),
            pltpu.VMEM((384, 192), b16),
            pltpu.VMEM((384, 64), b16),
            pltpu.VMEM((128, 64), b16),
            pltpu.VMEM((128, 64), b16),
            pltpu.VMEM((GROUP, 2, 64, quarter // 2), f32),
            pltpu.VMEM((GROUP, 2, 64, quarter // 2), f32),
            pltpu.VMEM((2, 64, quarter // 2), f32),
            pltpu.VMEM((GROUP, 2, 64, quarter // 2), f32),
            pltpu.VMEM((GROUP, 2, 64, quarter // 2), f32),
            pltpu.VMEM((1, 64, elements), f32),
            pltpu.VMEM((64, 64), f32),
            pltpu.VMEM((64, 96), f32),
            pltpu.VMEM((64, 64), f32),
            pltpu.VMEM((6, elements), i32),
            pltpu.VMEM((6, elements), i32),
            pltpu.VMEM((1, bound), i32),
            pltpu.VMEM((1, bound), i32),
            dma((8,)),
            dma((tiles,)),
            dma((STEPS, 2)),
            dma((STEPS, 2)),
            dma((GROUP - 1, 2)),
            dma((GROUP - 1, 2)),
            dma((2,)),
            dma((2,)),
            dma((GROUP - 1, 2)),
            dma((GROUP - 1, 2)),
        ],
        compiler_params=pltpu.CompilerParams(
            collective_id=0, has_side_effects=True, vmem_limit_bytes=40 * 1024 * 1024
        ),
    )(
        start_state, stiffness, lifting, coarse, neighbor, orientation,
        send_low.reshape(1, bound), send_high.reshape(1, bound),
    )


def solution(mesh):
    return jax.shard_map(
        shards,
        mesh=mesh,
        in_specs=(
            P("tm", None, "space"),
            P(),
            P(),
            P(),
            P(None, "space"),
            P(None, "space"),
            P("space"),
            P("space"),
        ),
        out_specs=P("tm", None, "space"),
        check_vma=False,
    )
```

```python
import functools

import jax
import jax.numpy as jnp
from jax import lax
from jax.experimental import pallas as pl
from jax.experimental.pallas import tpu as pltpu
from jax.sharding import PartitionSpec as P

STEPS = 3
GROUP = 4
LANES = 128
WIDE = 256
MESH = pl.DeviceIdType.MESH

time_step = 0.05


def exact(a, b):
    return jnp.dot(a, b, precision=lax.Precision.HIGHEST, preferred_element_type=jnp.float32)


def parts_of(value):
    head = value.astype(jnp.bfloat16)
    tail = (value - head.astype(jnp.float32)).astype(jnp.bfloat16)
    return head, tail


def keep_split(ref, value):
    rows = value.shape[0]
    head, tail = parts_of(value)
    ref[0:rows, :] = head
    ref[rows : 2 * rows, :] = tail


def split_dot(ref, value):
    rows = ref.shape[0] // 2
    head, tail = parts_of(value)
    both = jnp.dot(ref[...], head, preferred_element_type=jnp.float32)
    rest = jnp.dot(ref[0:rows, :], tail, preferred_element_type=jnp.float32)
    return both[:rows] + (both[rows:] + rest)


def along(value, index, axis):
    return jnp.take_along_axis(value, index, axis=axis, mode="promise_in_bounds")


def pick(sources, index, upper=None, lower=None):
    lane = index & (LANES - 1)
    tile = index >> 7
    for number, load in sources:
        first, second = load()
        first, second = along(first, lane, 1), along(second, lane, 1)
        if upper is None:
            upper, lower = first, second
        else:
            here = tile == number
            upper, lower = jnp.where(here, first, upper), jnp.where(here, second, lower)
    return upper, lower


def selection():
    row = lax.broadcasted_iota(jnp.int32, (96, 64), 0)
    node = lax.broadcasted_iota(jnp.int32, (96, 64), 1)
    face, a, b = row >> 4, (row >> 2) & 3, row & 3
    place = jnp.where(
        face < 2, 4 * a + b, jnp.where(face < 4, 16 * a + b, 16 * a + 4 * b)
    ) + jnp.where(face == 1, 48, jnp.where(face == 3, 12, jnp.where(face == 5, 3, 0)))
    return jnp.where(place == node, 1.0, 0.0).astype(jnp.float32)


def kernel(
    n_time, n_space,
    start_ref, stiff_ref, lift_ref, coarse_ref, near_ref, turn_ref, low_ref, high_ref,
    out_ref,
    stack, trace, heads, chosen, met, spot, coarse_start, leave, halo, joined, weights, reach, powers, last_power, one_power,
    defect, gathered, carry, ends, final,
    start_in, stiff_in, lift_in, coarse_in, near_in, turn_in, low_in, high_in, load_sem, state_sem,
    halo_send, halo_recv, mix_send, mix_recv, chain_send, chain_recv, back_send, back_recv,
):
    elements = start_ref.shape[2]
    loads = {}
    for number, (name, source, target) in enumerate(
        (
            ("low", low_ref, low_in),
            ("high", high_ref, high_in),
            ("turn", turn_ref, turn_in),
            ("stiff", stiff_ref, stiff_in),
            ("lift", lift_ref, lift_in),
            ("near", near_ref, near_in),
            ("coarse", coarse_ref, coarse_in),
            ("start", start_ref, start_in),
        )
    ):
        loads[name] = pltpu.make_async_copy(source, target, load_sem.at[number])
    for name in ("low", "high"):
        loads[name].start()
    states = []
    for tile in range(elements // LANES):
        states.append(
            pltpu.make_async_copy(
                start_ref.at[0, :, tile * LANES : (tile + 1) * LANES],
                stack.at[tile, 0:64, :],
                state_sem.at[tile],
            )
        )
        states[-1].start()
    for name in ("turn", "stiff", "lift", "near", "coarse", "start"):
        loads[name].start()
    tiles = elements // LANES
    bound = low_ref.shape[1]
    bound_tiles = bound // LANES
    quarter = elements // GROUP
    me_t, me_s = lax.axis_index("tm"), lax.axis_index("space")
    group, rank = me_t // GROUP, me_t % GROUP
    first = group * GROUP
    groups = n_time // GROUP
    below, above = (me_s + n_space - 1) % n_space, (me_s + 1) % n_space
    mates = [first + (rank + by) % GROUP for by in range(1, GROUP)]
    following = (me_t + GROUP) % n_time
    previous = (me_t + n_time - GROUP) % n_time

    barrier = pltpu.get_barrier_semaphore()
    for space in (below, above):
        pl.semaphore_signal(barrier, inc=1, device_id=(me_t, space), device_id_type=MESH)
    for time in mates + [following, previous]:
        pl.semaphore_signal(barrier, inc=1, device_id=(time, me_s), device_id_type=MESH)

    def keep_traces(tile):
        for i in range(4):
            trace[tile, 0, 4 * i : 4 * i + 4, :] = stack[tile, 16 * i : 16 * i + 4, :]
            trace[tile, 1, 4 * i : 4 * i + 4, :] = stack[tile, 16 * i + 12 : 16 * i + 16, :]
        trace[tile, 2] = stack[tile, pl.ds(0, 16, stride=4), :]
        trace[tile, 3] = stack[tile, pl.ds(3, 16, stride=4), :]
        for face in range(6):
            if face < 2:
                value = stack[tile, 48 * face : 48 * face + 16, :]
            else:
                value = trace[tile, face - 2]
            head, tail = parts_of(value)
            heads[face, 0:16, tile * LANES : (tile + 1) * LANES] = head
            heads[face, 16:32, tile * LANES : (tile + 1) * LANES] = tail

    loads["low"].wait()
    loads["high"].wait()
    for copy in states:
        copy.wait()

    def local_source(face, s):
        if face == 0:
            return s, lambda: (stack[s, 0:8, :], stack[s, 8:16, :])
        if face == 1:
            return s, lambda: (stack[s, 48:56, :], stack[s, 56:64, :])
        return s, lambda: (trace[s, face - 2, 0:8, :], trace[s, face - 2, 8:16, :])

    def wide_index(ref, row, t):
        at = pl.multiple_of(t * LANES, LANES)
        return jnp.broadcast_to(ref[row : row + 1, pl.ds(at, LANES)], (8, LANES))

    def halo_copies(step):
        return [
            pltpu.make_async_remote_copy(
                src_ref=leave.at[step, side],
                dst_ref=halo.at[step, side],
                send_sem=halo_send.at[step, side],
                recv_sem=halo_recv.at[step, side],
                device_id=(me_t, target),
                device_id_type=MESH,
            )
            for side, target in ((0, below), (1, above))
        ]

    def send_halo(step):
        def fill(t, _):
            for side, ref in ((0, low_in), (1, high_in)):
                sources = [local_source(side, s) for s in range(tiles)]
                upper, lower = pick(sources, wide_index(ref, 0, t))
                leave[step, side, t, 0:8, :] = upper
                leave[step, side, t, 8:16, :] = lower
            return 0

        lax.fori_loop(0, bound_tiles, fill, 0, unroll=4)
        if step == 0:
            pl.semaphore_wait(barrier, 2 + GROUP - 1 + 2)
        copies = halo_copies(step)
        for copy in copies:
            copy.start()
        return copies

    def place(face, t, upper, lower):
        for half in range(2):
            index = spot[face, t, 8 * half : 8 * half + 8, :]
            row = index & 7
            turned = jnp.where(index < 8, along(upper, row, 0), along(lower, row, 0))
            at = 64 + 16 * face + 8 * half
            stack[t, at : at + 8, :] = turned

    def choose(k, _):
        row = lax.broadcasted_iota(jnp.int32, (LANES, WIDE), 0) + k * LANES
        at = pl.multiple_of(k * LANES, LANES)
        for face in range(6):
            for c in range(elements // WIDE):
                index = near_in[face : face + 1, c * WIDE : (c + 1) * WIDE]
                hit = jnp.where(row == index, 1.0, 0.0).astype(jnp.bfloat16)
                chosen[face, c, pl.ds(at, LANES), :] = hit
        return 0

    def local_faces(c, _):
        for face in (2, 3, 4, 5, 0, 1):
            both = jnp.dot(heads[face ^ 1], chosen[face, c], preferred_element_type=jnp.float32)
            value = both[0:16] + both[16:32]
            for piece in range(WIDE // LANES):
                t = c * (WIDE // LANES) + piece
                part = value[:, piece * LANES : (piece + 1) * LANES]
                if face < 2:
                    met[face, t] = part
                else:
                    place(face, t, part[0:8], part[8:16])
        return 0

    def outer_faces(step):
        def body(t, _):
            for face in range(2):
                side = 1 - face
                sources = []
                for b in range(bound_tiles):
                    number = tiles + face * bound_tiles + b
                    sources.append(
                        (
                            number,
                            lambda b=b: (
                                halo[step, side, b, 0:8, :],
                                halo[step, side, b, 8:16, :],
                            ),
                        )
                    )
                inside = met[face, t, 0:8, :], met[face, t, 8:16, :]
                place(face, t, *pick(sources, wide_index(near_in, face, t), *inside))
            return 0

        return body

    copies = send_halo(0)

    def spots(t, _):
        row = lax.broadcasted_iota(jnp.int32, (16, LANES), 0)
        at = pl.multiple_of(t * LANES, LANES)
        for face in range(6):
            code = jnp.broadcast_to(turn_in[face : face + 1, pl.ds(at, LANES)], (16, LANES))
            a, b = row >> 2, row & 3
            a = jnp.where((code & 1) != 0, 3 - a, a)
            b = jnp.where((code & 2) != 0, 3 - b, b)
            spot[face, t] = jnp.where((code & 4) != 0, 4 * b + a, 4 * a + b)
        return 0

    loads["turn"].wait()
    lax.fori_loop(0, tiles, spots, 0)
    for tile in range(tiles):
        keep_traces(tile)

    def fine_matrix():
        loads["stiff"].wait()
        loads["lift"].wait()
        lifting = lift_in[...]
        row64 = lax.broadcasted_iota(jnp.int32, (64, 64), 0)
        col64 = lax.broadcasted_iota(jnp.int32, (64, 64), 1)
        unit = jnp.where(row64 == col64, 1.0, 0.0).astype(jnp.float32)
        joined[:, 0:64] = stiff_in[...] - exact(lifting, selection()) + unit
        joined[:, 64:160] = lifting
        keep_split(weights, joined[...])

    def coarse_matrices():
        loads["coarse"].wait()
        one = coarse_in[...]
        two = exact(one, one)
        three = exact(two, one)
        four = exact(two, two)
        keep_split(one_power, one)
        keep_split(last_power, four)
        for part in range(2):
            for at, power in enumerate((one, two, three)):
                value = parts_of(power)[part]
                powers[192 * part + 64 * at : 192 * part + 64 * at + 64, :] = value
        zero = jnp.zeros((64, 64), jnp.float32)
        table = ((one, zero, zero), (two, one, zero), (three, two, one))
        for i in range(3):
            line = jnp.concatenate(table[i], axis=1)
            head, tail = parts_of(line)
            reach[64 * i : 64 * i + 64, :] = head
            reach[192 + 64 * i : 256 + 64 * i, :] = tail

    def coarse_first():
        loads["start"].wait()
        for c in range(elements // WIDE):
            columns = start_in[0, :, c * WIDE : (c + 1) * WIDE]
            coarse_start[c] = jnp.where(me_t == 0, 0.0, split_dot(one_power, columns))

    def advance(c):
        operand = jnp.concatenate([stack[2 * c], stack[2 * c + 1]], axis=1)
        state = operand[0:64]
        rate = split_dot(weights, operand) - state * state * state
        return state + time_step * rate

    for step in range(STEPS):
        if step > 0:
            copies = send_halo(step)
            for tile in range(tiles):
                keep_traces(tile)
        if step == 0:
            fine_matrix()
            loads["near"].wait()
            lax.fori_loop(0, tiles, choose, 0)
        lax.fori_loop(0, elements // WIDE, local_faces, 0, unroll=2)
        if step == 1:
            coarse_matrices()
        if step == 2:
            coarse_first()
        for copy in copies:
            copy.wait()
        lax.fori_loop(0, tiles, outer_faces(step), 0, unroll=4)
        if step < STEPS - 1:
            for c in range(elements // WIDE):
                later = advance(c)
                stack[2 * c, 0:64, :] = later[:, :LANES]
                stack[2 * c + 1, 0:64, :] = later[:, LANES:]

    pairs = (None, rank + 1 - 2 * (rank % 2), (rank + 2) % GROUP, GROUP - 1 - rank)

    def swap(source, target, send, recv, by, half):
        other = pairs[by]
        return pltpu.make_async_remote_copy(
            src_ref=source.at[other, half],
            dst_ref=target.at[rank, half],
            send_sem=send.at[by - 1, half],
            recv_sem=recv.at[by - 1, half],
            device_id=(first + other, me_s),
            device_id_type=MESH,
        )

    def last_step(q, target, slot):
        for w in range(quarter // WIDE):
            c = q * (quarter // WIDE) + w
            value = advance(c) - coarse_start[c]
            for piece in range(2):
                at = w * WIDE + piece * LANES
                half, column = at // (quarter // 2), at % (quarter // 2)
                target[slot, half, :, column : column + LANES] = value[
                    :, piece * LANES : (piece + 1) * LANES
                ]

    mixes = {(by, h): swap(defect, gathered, mix_send, mix_recv, by, h) for by in (2, 3, 1) for h in (0, 1)}
    for by in (2, 3, 1):
        last_step(pairs[by], defect, pairs[by])
        mixes[by, 0].start()
    for by in (2, 3, 1):
        mixes[by, 1].start()
    last_step(rank, gathered, rank)

    chain = [
        pltpu.make_async_remote_copy(
            src_ref=ends.at[GROUP - 1, h],
            dst_ref=carry.at[h],
            send_sem=chain_send.at[h],
            recv_sem=chain_recv.at[h],
            device_id=(following, me_s),
            device_id_type=MESH,
        )
        for h in range(2)
    ]
    backs = {(by, h): swap(ends, final, back_send, back_recv, by, h) for by in (2, 3, 1) for h in (0, 1)}

    def give_back(h):
        for by in (2, 3, 1):
            backs[by, h].start()
        final[rank, h] = ends[rank, h]

    for h in range(2):
        for by in (1, 2, 3):
            mixes[by, h].wait_recv()
        inputs = jnp.concatenate([gathered[0, h], gathered[1, h], gathered[2, h]], axis=0)
        reached = split_dot(reach, inputs)
        ends[0, h] = gathered[0, h]
        for m in range(1, GROUP):
            ends[m, h] = gathered[m, h] + reached[64 * m - 64 : 64 * m]

        @pl.when(group == 0)
        def _():
            if groups > 1:
                chain[h].start()
            give_back(h)

    @pl.when(group > 0)
    def _():
        for h in range(2):
            chain[h].wait_recv()
            held = carry[h]
            ends[GROUP - 1, h] = ends[GROUP - 1, h] + split_dot(last_power, held)

            @pl.when(group < groups - 1)
            def _():
                chain[h].start()

            spread = split_dot(powers, held)
            for m in range(GROUP - 1):
                ends[m, h] = ends[m, h] + spread[64 * m : 64 * m + 64]
            give_back(h)

    for copy in mixes.values():
        copy.wait_send()

    @pl.when(group < groups - 1)
    def _():
        for h in range(2):
            chain[h].wait_send()

    for h in range(2):
        for by in (1, 2, 3):
            backs[by, h].wait()
        for q in range(GROUP):
            at = q * quarter + h * (quarter // 2)
            out_ref[0, :, at : at + quarter // 2] = final[q, h]


def shards(start_state, stiffness, lifting, coarse, neighbor, orientation, send_low, send_high):
    elements = start_state.shape[2]
    bound = send_low.shape[0]
    tiles, bound_tiles, quarter = elements // LANES, bound // LANES, elements // GROUP
    f32, b16, i32 = jnp.float32, jnp.bfloat16, jnp.int32
    dma = pltpu.SemaphoreType.DMA
    vmem = pl.BlockSpec(memory_space=pltpu.VMEM)
    return pl.pallas_call(
        functools.partial(kernel, lax.axis_size("tm"), lax.axis_size("space")),
        out_shape=jax.ShapeDtypeStruct(start_state.shape, f32),
        in_specs=[pl.BlockSpec(memory_space=pltpu.HBM)] * 8,
        out_specs=vmem,
        scratch_shapes=[
            pltpu.VMEM((tiles, 160, LANES), f32),
            pltpu.VMEM((tiles, 4, 16, LANES), f32),
            pltpu.VMEM((6, 32, elements), b16),
            pltpu.VMEM((6, elements // WIDE, elements, WIDE), b16),
            pltpu.VMEM((2, tiles, 16, LANES), f32),
            pltpu.VMEM((6, tiles, 16, LANES), i32),
            pltpu.VMEM((elements // WIDE, 64, WIDE), f32),
            pltpu.VMEM((STEPS, 2, bound_tiles, 16, LANES), f32),
            pltpu.VMEM((STEPS, 2, bound_tiles, 16, LANES), f32),
            pltpu.VMEM((64, 160), f32),
            pltpu.VMEM((128, 160), b16),
            pltpu.VMEM((384, 192), b16),
            pltpu.VMEM((384, 64), b16),
            pltpu.VMEM((128, 64), b16),
            pltpu.VMEM((128, 64), b16),
            pltpu.VMEM((GROUP, 2, 64, quarter // 2), f32),
            pltpu.VMEM((GROUP, 2, 64, quarter // 2), f32),
            pltpu.VMEM((2, 64, quarter // 2), f32),
            pltpu.VMEM((GROUP, 2, 64, quarter // 2), f32),
            pltpu.VMEM((GROUP, 2, 64, quarter // 2), f32),
            pltpu.VMEM((1, 64, elements), f32),
            pltpu.VMEM((64, 64), f32),
            pltpu.VMEM((64, 96), f32),
            pltpu.VMEM((64, 64), f32),
            pltpu.VMEM((6, elements), i32),
            pltpu.VMEM((6, elements), i32),
            pltpu.VMEM((1, bound), i32),
            pltpu.VMEM((1, bound), i32),
            dma((8,)),
            dma((tiles,)),
            dma((STEPS, 2)),
            dma((STEPS, 2)),
            dma((GROUP - 1, 2)),
            dma((GROUP - 1, 2)),
            dma((2,)),
            dma((2,)),
            dma((GROUP - 1, 2)),
            dma((GROUP - 1, 2)),
        ],
        compiler_params=pltpu.CompilerParams(
            collective_id=0, has_side_effects=True, vmem_limit_bytes=63 * 1024 * 1024
        ),
    )(
        start_state, stiffness, lifting, coarse, neighbor, orientation,
        send_low.reshape(1, bound), send_high.reshape(1, bound),
    )


def solution(mesh):
    return jax.shard_map(
        shards,
        mesh=mesh,
        in_specs=(
            P("tm", None, "space"),
            P(),
            P(),
            P(),
            P(None, "space"),
            P(None, "space"),
            P("space"),
            P("space"),
        ),
        out_specs=P("tm", None, "space"),
        check_vma=False,
    )
```

```python
import functools

import jax
import jax.numpy as jnp
from jax import lax
from jax.experimental import pallas as pl
from jax.experimental.pallas import tpu as pltpu
from jax.sharding import PartitionSpec as P

STEPS = 3
GROUP = 4
LANES = 128
WIDE = 256
MESH = pl.DeviceIdType.MESH

time_step = 0.05


def exact(a, b):
    return jnp.dot(a, b, precision=lax.Precision.HIGHEST, preferred_element_type=jnp.float32)


def parts_of(value):
    head = value.astype(jnp.bfloat16)
    tail = (value - head.astype(jnp.float32)).astype(jnp.bfloat16)
    return head, tail


def keep_split(ref, value):
    rows = value.shape[0]
    head, tail = parts_of(value)
    ref[0:rows, :] = head
    ref[rows : 2 * rows, :] = tail


def split_dot(ref, value):
    rows = ref.shape[0] // 2
    head, tail = parts_of(value)
    both = jnp.dot(ref[...], head, preferred_element_type=jnp.float32)
    rest = jnp.dot(ref[0:rows, :], tail, preferred_element_type=jnp.float32)
    return both[:rows] + (both[rows:] + rest)


def along(value, index, axis):
    return jnp.take_along_axis(value, index, axis=axis, mode="promise_in_bounds")


def pick(sources, index, upper=None, lower=None):
    lane = index & (LANES - 1)
    tile = index >> 7
    for number, load in sources:
        first, second = load()
        first, second = along(first, lane, 1), along(second, lane, 1)
        if upper is None:
            upper, lower = first, second
        else:
            here = tile == number
            upper, lower = jnp.where(here, first, upper), jnp.where(here, second, lower)
    return upper, lower


def selection():
    row = lax.broadcasted_iota(jnp.int32, (96, 64), 0)
    node = lax.broadcasted_iota(jnp.int32, (96, 64), 1)
    face, a, b = row >> 4, (row >> 2) & 3, row & 3
    place = jnp.where(
        face < 2, 4 * a + b, jnp.where(face < 4, 16 * a + b, 16 * a + 4 * b)
    ) + jnp.where(face == 1, 48, jnp.where(face == 3, 12, jnp.where(face == 5, 3, 0)))
    return jnp.where(place == node, 1.0, 0.0).astype(jnp.float32)


def kernel(
    n_time, n_space,
    start_ref, stiff_ref, lift_ref, coarse_ref, near_ref, turn_ref, low_ref, high_ref,
    out_ref,
    stack, trace, heads, chosen, send_hot, meet_hot, met, spot, coarse_start, leave, halo, joined, weights, reach, powers, last_power, one_power,
    defect, gathered, carry, ends, final,
    start_in, stiff_in, lift_in, coarse_in, near_in, turn_in, low_in, high_in, load_sem, state_sem,
    halo_send, halo_recv, mix_send, mix_recv, chain_send, chain_recv, back_send, back_recv,
):
    elements = start_ref.shape[2]
    loads = {}
    for number, (name, source, target) in enumerate(
        (
            ("low", low_ref, low_in),
            ("high", high_ref, high_in),
            ("turn", turn_ref, turn_in),
            ("stiff", stiff_ref, stiff_in),
            ("lift", lift_ref, lift_in),
            ("near", near_ref, near_in),
            ("coarse", coarse_ref, coarse_in),
            ("start", start_ref, start_in),
        )
    ):
        loads[name] = pltpu.make_async_copy(source, target, load_sem.at[number])
    for name in ("low", "high"):
        loads[name].start()
    states = []
    for tile in range(elements // LANES):
        states.append(
            pltpu.make_async_copy(
                start_ref.at[0, :, tile * LANES : (tile + 1) * LANES],
                stack.at[tile, 0:64, :],
                state_sem.at[tile],
            )
        )
        states[-1].start()
    for name in ("turn", "stiff", "lift", "near", "coarse", "start"):
        loads[name].start()
    small = elements <= 1024
    tiles = elements // LANES
    bound = low_ref.shape[1]
    bound_tiles = bound // LANES
    quarter = elements // GROUP
    me_t, me_s = lax.axis_index("tm"), lax.axis_index("space")
    group, rank = me_t // GROUP, me_t % GROUP
    first = group * GROUP
    groups = n_time // GROUP
    below, above = (me_s + n_space - 1) % n_space, (me_s + 1) % n_space
    mates = [first + (rank + by) % GROUP for by in range(1, GROUP)]
    following = (me_t + GROUP) % n_time
    previous = (me_t + n_time - GROUP) % n_time

    barrier = pltpu.get_barrier_semaphore()
    for space in (below, above):
        pl.semaphore_signal(barrier, inc=1, device_id=(me_t, space), device_id_type=MESH)
    for time in mates + [following, previous]:
        pl.semaphore_signal(barrier, inc=1, device_id=(time, me_s), device_id_type=MESH)

    def keep_parts(face, tile, value):
        head, tail = parts_of(value)
        heads[face, 0:16, tile * LANES : (tile + 1) * LANES] = head
        heads[face, 16:32, tile * LANES : (tile + 1) * LANES] = tail

    def keep_outer(tile):
        for face in range(2):
            keep_parts(face, tile, stack[tile, 48 * face : 48 * face + 16, :])

    def keep_inner(tile):
        for i in range(4):
            trace[tile, 0, 4 * i : 4 * i + 4, :] = stack[tile, 16 * i : 16 * i + 4, :]
            trace[tile, 1, 4 * i : 4 * i + 4, :] = stack[tile, 16 * i + 12 : 16 * i + 16, :]
        trace[tile, 2] = stack[tile, pl.ds(0, 16, stride=4), :]
        trace[tile, 3] = stack[tile, pl.ds(3, 16, stride=4), :]
        for face in range(2, 6):
            keep_parts(face, tile, trace[tile, face - 2])

    loads["low"].wait()
    loads["high"].wait()
    for copy in states:
        copy.wait()

    def local_source(face, s):
        if face == 0:
            return s, lambda: (stack[s, 0:8, :], stack[s, 8:16, :])
        if face == 1:
            return s, lambda: (stack[s, 48:56, :], stack[s, 56:64, :])
        return s, lambda: (trace[s, face - 2, 0:8, :], trace[s, face - 2, 8:16, :])

    def wide_index(ref, row, t):
        at = pl.multiple_of(t * LANES, LANES)
        return jnp.broadcast_to(ref[row : row + 1, pl.ds(at, LANES)], (8, LANES))

    def halo_copies(step):
        return [
            pltpu.make_async_remote_copy(
                src_ref=leave.at[step, side],
                dst_ref=halo.at[step, side],
                send_sem=halo_send.at[step, side],
                recv_sem=halo_recv.at[step, side],
                device_id=(me_t, target),
                device_id_type=MESH,
            )
            for side, target in ((0, below), (1, above))
        ]

    def send_halo(step):
        def fill(t, _):
            for side, ref in ((0, low_in), (1, high_in)):
                sources = [local_source(side, s) for s in range(tiles)]
                upper, lower = pick(sources, wide_index(ref, 0, t))
                leave[step, side, t, 0:8, :] = upper
                leave[step, side, t, 8:16, :] = lower
            return 0

        if step == 0 or not small:
            lax.fori_loop(0, bound_tiles, fill, 0, unroll=4)
        else:
            for side in range(2):
                both = jnp.dot(heads[side], send_hot[side], preferred_element_type=jnp.float32)
                value = both[0:16] + both[16:32]
                for b in range(bound_tiles):
                    leave[step, side, b] = value[:, b * LANES : (b + 1) * LANES]
        if step == 0:
            pl.semaphore_wait(barrier, 2 + GROUP - 1 + 2)
        copies = halo_copies(step)
        for copy in copies:
            copy.start()
        return copies

    def place(face, t, upper, lower):
        for half in range(2):
            index = spot[face, t, 8 * half : 8 * half + 8, :]
            row = index & 7
            turned = jnp.where(index < 8, along(upper, row, 0), along(lower, row, 0))
            at = 64 + 16 * face + 8 * half
            stack[t, at : at + 8, :] = turned

    def one_hot(index, k):
        row = lax.broadcasted_iota(jnp.int32, (LANES, index.shape[1]), 0)
        row = row.astype(jnp.float32).astype(jnp.bfloat16)
        inside = jnp.clip(index - k * LANES, -1, LANES).astype(jnp.float32).astype(jnp.bfloat16)
        inside = jnp.broadcast_to(inside, row.shape)
        return jnp.where(row == inside, jnp.ones_like(row), jnp.zeros_like(row))

    def choose(k, _):
        at = pl.ds(pl.multiple_of(k * LANES, LANES), LANES)
        for face in range(6):
            for c in range(elements // WIDE):
                index = near_in[face : face + 1, c * WIDE : (c + 1) * WIDE]
                chosen[face, c, at, :] = one_hot(index, k)
        return 0

    def choose_sent(k, _):
        at = pl.ds(pl.multiple_of(k * LANES, LANES), LANES)
        for side, ref in ((0, low_in), (1, high_in)):
            send_hot[side, at, :] = one_hot(ref[...], k)
        return 0

    def choose_met(k, _):
        at = pl.ds(pl.multiple_of(k * LANES, LANES), LANES)
        for face in range(2):
            for c in range(elements // WIDE):
                index = near_in[face : face + 1, c * WIDE : (c + 1) * WIDE]
                meet_hot[face, c, at, :] = one_hot(index - (elements + face * bound), k)
        return 0

    def halo_parts(step, face):
        tiles_in = [halo[step, 1 - face, b] for b in range(bound_tiles)]
        head, tail = parts_of(jnp.concatenate(tiles_in, axis=1))
        return jnp.concatenate([head, tail], axis=0)

    def meet(c, parts):
        for face in range(2):
            both = jnp.dot(parts[face], meet_hot[face, c], preferred_element_type=jnp.float32)
            value = both[0:16] + both[16:32]
            for piece in range(WIDE // LANES):
                t = c * (WIDE // LANES) + piece
                part = met[face, t] + value[:, piece * LANES : (piece + 1) * LANES]
                place(face, t, part[0:8], part[8:16])

    def local_faces(c, _):
        for face in (2, 3, 4, 5, 0, 1):
            both = jnp.dot(heads[face ^ 1], chosen[face, c], preferred_element_type=jnp.float32)
            value = both[0:16] + both[16:32]
            for piece in range(WIDE // LANES):
                t = c * (WIDE // LANES) + piece
                part = value[:, piece * LANES : (piece + 1) * LANES]
                if face < 2:
                    met[face, t] = part
                else:
                    place(face, t, part[0:8], part[8:16])
        return 0

    def outer_faces(step):
        def body(t, _):
            for face in range(2):
                side = 1 - face
                sources = []
                for b in range(bound_tiles):
                    number = tiles + face * bound_tiles + b
                    sources.append(
                        (
                            number,
                            lambda b=b: (
                                halo[step, side, b, 0:8, :],
                                halo[step, side, b, 8:16, :],
                            ),
                        )
                    )
                inside = met[face, t, 0:8, :], met[face, t, 8:16, :]
                place(face, t, *pick(sources, wide_index(near_in, face, t), *inside))
            return 0

        return body

    copies = send_halo(0)

    def spots(t, _):
        row = lax.broadcasted_iota(jnp.int32, (16, LANES), 0)
        at = pl.multiple_of(t * LANES, LANES)
        for face in range(6):
            code = jnp.broadcast_to(turn_in[face : face + 1, pl.ds(at, LANES)], (16, LANES))
            a, b = row >> 2, row & 3
            a = jnp.where((code & 1) != 0, 3 - a, a)
            b = jnp.where((code & 2) != 0, 3 - b, b)
            spot[face, t] = jnp.where((code & 4) != 0, 4 * b + a, 4 * a + b)
        return 0

    loads["turn"].wait()
    lax.fori_loop(0, tiles, spots, 0)
    for tile in range(tiles):
        keep_outer(tile)
        keep_inner(tile)

    def fine_matrix():
        loads["stiff"].wait()
        loads["lift"].wait()
        lifting = lift_in[...]
        row64 = lax.broadcasted_iota(jnp.int32, (64, 64), 0)
        col64 = lax.broadcasted_iota(jnp.int32, (64, 64), 1)
        unit = jnp.where(row64 == col64, 1.0, 0.0).astype(jnp.float32)
        joined[:, 0:64] = stiff_in[...] - exact(lifting, selection()) + unit
        joined[:, 64:160] = lifting
        keep_split(weights, joined[...])

    def coarse_matrices():
        loads["coarse"].wait()
        one = coarse_in[...]
        two = exact(one, one)
        three = exact(two, one)
        four = exact(two, two)
        keep_split(one_power, one)
        keep_split(last_power, four)
        for part in range(2):
            for at, power in enumerate((one, two, three)):
                value = parts_of(power)[part]
                powers[192 * part + 64 * at : 192 * part + 64 * at + 64, :] = value
        zero = jnp.zeros((64, 64), jnp.float32)
        table = ((one, zero, zero), (two, one, zero), (three, two, one))
        for i in range(3):
            line = jnp.concatenate(table[i], axis=1)
            head, tail = parts_of(line)
            reach[64 * i : 64 * i + 64, :] = head
            reach[192 + 64 * i : 256 + 64 * i, :] = tail

    def coarse_first():
        loads["start"].wait()
        for c in range(elements // WIDE):
            columns = start_in[0, :, c * WIDE : (c + 1) * WIDE]
            coarse_start[c] = jnp.where(me_t == 0, 0.0, split_dot(one_power, columns))

    def advance(c):
        operand = jnp.concatenate([stack[2 * c], stack[2 * c + 1]], axis=1)
        state = operand[0:64]
        rate = split_dot(weights, operand) - state * state * state
        return state + time_step * rate

    for step in range(STEPS):
        if step > 0:
            for tile in range(tiles):
                keep_outer(tile)
            copies = send_halo(step)
            for tile in range(tiles):
                keep_inner(tile)
        if step == 0:
            fine_matrix()
            loads["near"].wait()
            lax.fori_loop(0, tiles, choose, 0)
            if small:
                lax.fori_loop(0, bound_tiles, choose_met, 0)
                lax.fori_loop(0, tiles, choose_sent, 0)
        lax.fori_loop(0, elements // WIDE, local_faces, 0, unroll=2)
        if step == 1:
            coarse_matrices()
        if step == 2:
            coarse_first()
        for copy in copies:
            copy.wait()
        if small:
            parts = [halo_parts(step, face) for face in range(2)]
            for c in range(elements // WIDE):
                meet(c, parts)
        else:
            lax.fori_loop(0, tiles, outer_faces(step), 0, unroll=4)
        if step < STEPS - 1:
            for c in range(elements // WIDE):
                later = advance(c)
                stack[2 * c, 0:64, :] = later[:, :LANES]
                stack[2 * c + 1, 0:64, :] = later[:, LANES:]

    pairs = (None, rank + 1 - 2 * (rank % 2), (rank + 2) % GROUP, GROUP - 1 - rank)

    def swap(source, target, send, recv, by, half):
        other = pairs[by]
        return pltpu.make_async_remote_copy(
            src_ref=source.at[other, half],
            dst_ref=target.at[rank, half],
            send_sem=send.at[by - 1, half],
            recv_sem=recv.at[by - 1, half],
            device_id=(first + other, me_s),
            device_id_type=MESH,
        )

    def last_step(q, target, slot):
        for w in range(quarter // WIDE):
            c = q * (quarter // WIDE) + w
            value = advance(c) - coarse_start[c]
            for piece in range(2):
                at = w * WIDE + piece * LANES
                half, column = at // (quarter // 2), at % (quarter // 2)
                target[slot, half, :, column : column + LANES] = value[
                    :, piece * LANES : (piece + 1) * LANES
                ]

    mixes = {(by, h): swap(defect, gathered, mix_send, mix_recv, by, h) for by in (2, 3, 1) for h in (0, 1)}
    for by in (2, 3, 1):
        last_step(pairs[by], defect, pairs[by])
        mixes[by, 0].start()
    for by in (2, 3, 1):
        mixes[by, 1].start()
    last_step(rank, gathered, rank)

    chain = [
        pltpu.make_async_remote_copy(
            src_ref=ends.at[GROUP - 1, h],
            dst_ref=carry.at[h],
            send_sem=chain_send.at[h],
            recv_sem=chain_recv.at[h],
            device_id=(following, me_s),
            device_id_type=MESH,
        )
        for h in range(2)
    ]
    backs = {(by, h): swap(ends, final, back_send, back_recv, by, h) for by in (2, 3, 1) for h in (0, 1)}

    def give_back(h):
        for by in (2, 3, 1):
            backs[by, h].start()
        final[rank, h] = ends[rank, h]

    for h in range(2):
        for by in (1, 2, 3):
            mixes[by, h].wait_recv()
        inputs = jnp.concatenate([gathered[0, h], gathered[1, h], gathered[2, h]], axis=0)
        reached = split_dot(reach, inputs)
        ends[0, h] = gathered[0, h]
        for m in range(1, GROUP):
            ends[m, h] = gathered[m, h] + reached[64 * m - 64 : 64 * m]

        @pl.when(group == 0)
        def _():
            if groups > 1:
                chain[h].start()
            give_back(h)

    @pl.when(group > 0)
    def _():
        for h in range(2):
            chain[h].wait_recv()
            held = carry[h]
            ends[GROUP - 1, h] = ends[GROUP - 1, h] + split_dot(last_power, held)

            @pl.when(group < groups - 1)
            def _():
                chain[h].start()

            spread = split_dot(powers, held)
            for m in range(GROUP - 1):
                ends[m, h] = ends[m, h] + spread[64 * m : 64 * m + 64]
            give_back(h)

    for copy in mixes.values():
        copy.wait_send()

    @pl.when(group < groups - 1)
    def _():
        for h in range(2):
            chain[h].wait_send()

    for h in range(2):
        for by in (1, 2, 3):
            backs[by, h].wait()
        for q in range(GROUP):
            at = q * quarter + h * (quarter // 2)
            out_ref[0, :, at : at + quarter // 2] = final[q, h]


def shards(start_state, stiffness, lifting, coarse, neighbor, orientation, send_low, send_high):
    elements = start_state.shape[2]
    bound = send_low.shape[0]
    tiles, bound_tiles, quarter = elements // LANES, bound // LANES, elements // GROUP
    f32, b16, i32 = jnp.float32, jnp.bfloat16, jnp.int32
    dma = pltpu.SemaphoreType.DMA
    vmem = pl.BlockSpec(memory_space=pltpu.VMEM)
    return pl.pallas_call(
        functools.partial(kernel, lax.axis_size("tm"), lax.axis_size("space")),
        out_shape=jax.ShapeDtypeStruct(start_state.shape, f32),
        in_specs=[pl.BlockSpec(memory_space=pltpu.HBM)] * 8,
        out_specs=vmem,
        scratch_shapes=[
            pltpu.VMEM((tiles, 160, LANES), f32),
            pltpu.VMEM((tiles, 4, 16, LANES), f32),
            pltpu.VMEM((6, 32, elements), b16),
            pltpu.VMEM((6, elements // WIDE, elements, WIDE), b16),
            pltpu.VMEM((2, elements, bound) if elements <= 1024 else (1, 16, LANES), b16),
            pltpu.VMEM((2, elements // WIDE, bound, WIDE) if elements <= 1024 else (1, 1, 16, LANES), b16),
            pltpu.VMEM((2, tiles, 16, LANES), f32),
            pltpu.VMEM((6, tiles, 16, LANES), i32),
            pltpu.VMEM((elements // WIDE, 64, WIDE), f32),
            pltpu.VMEM((STEPS, 2, bound_tiles, 16, LANES), f32),
            pltpu.VMEM((STEPS, 2, bound_tiles, 16, LANES), f32),
            pltpu.VMEM((64, 160), f32),
            pltpu.VMEM((128, 160), b16),
            pltpu.VMEM((384, 192), b16),
            pltpu.VMEM((384, 64), b16),
            pltpu.VMEM((128, 64), b16),
            pltpu.VMEM((128, 64), b16),
            pltpu.VMEM((GROUP, 2, 64, quarter // 2), f32),
            pltpu.VMEM((GROUP, 2, 64, quarter // 2), f32),
            pltpu.VMEM((2, 64, quarter // 2), f32),
            pltpu.VMEM((GROUP, 2, 64, quarter // 2), f32),
            pltpu.VMEM((GROUP, 2, 64, quarter // 2), f32),
            pltpu.VMEM((1, 64, elements), f32),
            pltpu.VMEM((64, 64), f32),
            pltpu.VMEM((64, 96), f32),
            pltpu.VMEM((64, 64), f32),
            pltpu.VMEM((6, elements), i32),
            pltpu.VMEM((6, elements), i32),
            pltpu.VMEM((1, bound), i32),
            pltpu.VMEM((1, bound), i32),
            dma((8,)),
            dma((tiles,)),
            dma((STEPS, 2)),
            dma((STEPS, 2)),
            dma((GROUP - 1, 2)),
            dma((GROUP - 1, 2)),
            dma((2,)),
            dma((2,)),
            dma((GROUP - 1, 2)),
            dma((GROUP - 1, 2)),
        ],
        compiler_params=pltpu.CompilerParams(
            collective_id=0, has_side_effects=True, vmem_limit_bytes=63 * 1024 * 1024
        ),
    )(
        start_state, stiffness, lifting, coarse, neighbor, orientation,
        send_low.reshape(1, bound), send_high.reshape(1, bound),
    )


def solution(mesh):
    return jax.shard_map(
        shards,
        mesh=mesh,
        in_specs=(
            P("tm", None, "space"),
            P(),
            P(),
            P(),
            P(None, "space"),
            P(None, "space"),
            P("space"),
            P("space"),
        ),
        out_specs=P("tm", None, "space"),
        check_vma=False,
    )
```

```python
import functools

import jax
import jax.numpy as jnp
from jax import lax
from jax.experimental import pallas as pl
from jax.experimental.pallas import tpu as pltpu
from jax.sharding import PartitionSpec as P

STEPS = 3
GROUP = 4
LANES = 128
WIDE = 256
MESH = pl.DeviceIdType.MESH

time_step = 0.05


def exact(a, b):
    return jnp.dot(a, b, precision=lax.Precision.HIGHEST, preferred_element_type=jnp.float32)


def parts_of(value):
    head = value.astype(jnp.bfloat16)
    tail = (value - head.astype(jnp.float32)).astype(jnp.bfloat16)
    return head, tail


def keep_split(ref, value):
    rows = value.shape[0]
    head, tail = parts_of(value)
    ref[0:rows, :] = head
    ref[rows : 2 * rows, :] = tail


def split_dot(ref, value):
    rows = ref.shape[0] // 2
    head, tail = parts_of(value)
    both = jnp.dot(ref[...], head, preferred_element_type=jnp.float32)
    rest = jnp.dot(ref[0:rows, :], tail, preferred_element_type=jnp.float32)
    return both[:rows] + (both[rows:] + rest)


def along(value, index, axis):
    return jnp.take_along_axis(value, index, axis=axis, mode="promise_in_bounds")


def pick(sources, index, upper=None, lower=None):
    lane = index & (LANES - 1)
    tile = index >> 7
    for number, load in sources:
        first, second = load()
        first, second = along(first, lane, 1), along(second, lane, 1)
        if upper is None:
            upper, lower = first, second
        else:
            here = tile == number
            upper, lower = jnp.where(here, first, upper), jnp.where(here, second, lower)
    return upper, lower


def selection():
    row = lax.broadcasted_iota(jnp.int32, (96, 64), 0)
    node = lax.broadcasted_iota(jnp.int32, (96, 64), 1)
    face, a, b = row >> 4, (row >> 2) & 3, row & 3
    place = jnp.where(
        face < 2, 4 * a + b, jnp.where(face < 4, 16 * a + b, 16 * a + 4 * b)
    ) + jnp.where(face == 1, 48, jnp.where(face == 3, 12, jnp.where(face == 5, 3, 0)))
    return jnp.where(place == node, 1.0, 0.0).astype(jnp.float32)


def kernel(
    n_time, n_space,
    start_ref, stiff_ref, lift_ref, coarse_ref, near_ref, turn_ref, low_ref, high_ref,
    out_ref,
    stack, trace, heads, chosen, send_hot, meet_hot, met, spot, coarse_start, leave, halo, joined, weights, reach, powers, last_power, one_power,
    defect, gathered, carry, ends, final,
    start_in, stiff_in, lift_in, coarse_in, near_in, turn_in, low_in, high_in, load_sem, state_sem,
    halo_send, halo_recv, mix_send, mix_recv, chain_send, chain_recv, back_send, back_recv,
):
    elements = start_ref.shape[2]
    loads = {}
    for number, (name, source, target) in enumerate(
        (
            ("low", low_ref, low_in),
            ("high", high_ref, high_in),
            ("turn", turn_ref, turn_in),
            ("stiff", stiff_ref, stiff_in),
            ("lift", lift_ref, lift_in),
            ("near", near_ref, near_in),
            ("coarse", coarse_ref, coarse_in),
            ("start", start_ref, start_in),
        )
    ):
        loads[name] = pltpu.make_async_copy(source, target, load_sem.at[number])
    for name in ("low", "high"):
        loads[name].start()
    states = []
    for tile in range(elements // LANES):
        states.append(
            pltpu.make_async_copy(
                start_ref.at[0, :, tile * LANES : (tile + 1) * LANES],
                stack.at[tile, 0:64, :],
                state_sem.at[tile],
            )
        )
        states[-1].start()
    for name in ("turn", "stiff", "lift", "near", "coarse", "start"):
        loads[name].start()
    small = elements <= 1024
    by_product, by_gather = (1, 3, 4, 5), (0, 2)
    tiles = elements // LANES
    bound = low_ref.shape[1]
    bound_tiles = bound // LANES
    quarter = elements // GROUP
    me_t, me_s = lax.axis_index("tm"), lax.axis_index("space")
    group, rank = me_t // GROUP, me_t % GROUP
    first = group * GROUP
    groups = n_time // GROUP
    below, above = (me_s + n_space - 1) % n_space, (me_s + 1) % n_space
    mates = [first + (rank + by) % GROUP for by in range(1, GROUP)]
    following = (me_t + GROUP) % n_time
    previous = (me_t + n_time - GROUP) % n_time

    barrier = pltpu.get_barrier_semaphore()
    for space in (below, above):
        pl.semaphore_signal(barrier, inc=1, device_id=(me_t, space), device_id_type=MESH)
    for time in mates + [following, previous]:
        pl.semaphore_signal(barrier, inc=1, device_id=(time, me_s), device_id_type=MESH)

    def keep_parts(face, tile, value):
        head, tail = parts_of(value)
        heads[face, 0:16, tile * LANES : (tile + 1) * LANES] = head
        heads[face, 16:32, tile * LANES : (tile + 1) * LANES] = tail

    def keep_outer(tile):
        for face in range(2):
            keep_parts(face, tile, stack[tile, 48 * face : 48 * face + 16, :])

    def keep_inner(tile):
        for i in range(4):
            trace[tile, 0, 4 * i : 4 * i + 4, :] = stack[tile, 16 * i : 16 * i + 4, :]
            trace[tile, 1, 4 * i : 4 * i + 4, :] = stack[tile, 16 * i + 12 : 16 * i + 16, :]
        trace[tile, 2] = stack[tile, pl.ds(0, 16, stride=4), :]
        trace[tile, 3] = stack[tile, pl.ds(3, 16, stride=4), :]
        for face in range(2, 6):
            keep_parts(face, tile, trace[tile, face - 2])

    loads["low"].wait()
    loads["high"].wait()
    for copy in states:
        copy.wait()

    def local_source(face, s):
        if face == 0:
            return s, lambda: (stack[s, 0:8, :], stack[s, 8:16, :])
        if face == 1:
            return s, lambda: (stack[s, 48:56, :], stack[s, 56:64, :])
        return s, lambda: (trace[s, face - 2, 0:8, :], trace[s, face - 2, 8:16, :])

    def wide_index(ref, row, t):
        at = pl.multiple_of(t * LANES, LANES)
        return jnp.broadcast_to(ref[row : row + 1, pl.ds(at, LANES)], (8, LANES))

    def halo_copies(step):
        return [
            pltpu.make_async_remote_copy(
                src_ref=leave.at[step, side],
                dst_ref=halo.at[step, side],
                send_sem=halo_send.at[step, side],
                recv_sem=halo_recv.at[step, side],
                device_id=(me_t, target),
                device_id_type=MESH,
            )
            for side, target in ((0, below), (1, above))
        ]

    def send_halo(step):
        def fill(side, ref, t):
            sources = [local_source(side, s) for s in range(tiles)]
            upper, lower = pick(sources, wide_index(ref, 0, t))
            leave[step, side, t, 0:8, :] = upper
            leave[step, side, t, 8:16, :] = lower

        both_sides = step == 0 or not small
        if not both_sides:
            both = jnp.dot(heads[1], send_hot[...], preferred_element_type=jnp.float32)
            value = both[0:16] + both[16:32]
            for b in range(bound_tiles):
                leave[step, 1, b] = value[:, b * LANES : (b + 1) * LANES]
        for t in range(bound_tiles):
            fill(0, low_in, t)
            if both_sides:
                fill(1, high_in, t)
        if step == 0:
            pl.semaphore_wait(barrier, 2 + GROUP - 1 + 2)
        copies = halo_copies(step)
        for copy in copies:
            copy.start()
        return copies

    def place(face, t, upper, lower):
        for half in range(2):
            index = spot[face, t, 8 * half : 8 * half + 8, :]
            row = index & 7
            turned = jnp.where(index < 8, along(upper, row, 0), along(lower, row, 0))
            at = 64 + 16 * face + 8 * half
            stack[t, at : at + 8, :] = turned

    def one_hot(index, k):
        row = lax.broadcasted_iota(jnp.int32, (LANES, index.shape[1]), 0)
        row = row.astype(jnp.float32).astype(jnp.bfloat16)
        inside = jnp.clip(index - k * LANES, -1, LANES).astype(jnp.float32).astype(jnp.bfloat16)
        inside = jnp.broadcast_to(inside, row.shape)
        return jnp.where(row == inside, jnp.ones_like(row), jnp.zeros_like(row))

    def choose(k, _):
        at = pl.ds(pl.multiple_of(k * LANES, LANES), LANES)
        for number, face in enumerate(by_product):
            for c in range(elements // WIDE):
                index = near_in[face : face + 1, c * WIDE : (c + 1) * WIDE]
                chosen[number, c, at, :] = one_hot(index, k)
        return 0

    def choose_sent(k, _):
        at = pl.ds(pl.multiple_of(k * LANES, LANES), LANES)
        send_hot[at, :] = one_hot(high_in[...], k)
        return 0

    def choose_met(k, _):
        at = pl.ds(pl.multiple_of(k * LANES, LANES), LANES)
        for c in range(elements // WIDE):
            index = near_in[1:2, c * WIDE : (c + 1) * WIDE]
            meet_hot[c, at, :] = one_hot(index - (elements + bound), k)
        return 0

    def halo_parts(step, face):
        tiles_in = [halo[step, 1 - face, b] for b in range(bound_tiles)]
        head, tail = parts_of(jnp.concatenate(tiles_in, axis=1))
        return jnp.concatenate([head, tail], axis=0)

    def halo_sources(step, face):
        sources = []
        for b in range(bound_tiles):
            number = tiles + face * bound_tiles + b
            sources.append(
                (
                    number,
                    lambda b=b: (
                        halo[step, 1 - face, b, 0:8, :],
                        halo[step, 1 - face, b, 8:16, :],
                    ),
                )
            )
        return sources

    def meet_gather(step, face, t):
        inside = met[face, t, 0:8, :], met[face, t, 8:16, :]
        index = wide_index(near_in, face, t)
        place(face, t, *pick(halo_sources(step, face), index, *inside))

    def meet(step, c, parts):
        both = jnp.dot(parts, meet_hot[c], preferred_element_type=jnp.float32)
        value = both[0:16] + both[16:32]
        for piece in range(WIDE // LANES):
            t = c * (WIDE // LANES) + piece
            part = met[1, t] + value[:, piece * LANES : (piece + 1) * LANES]
            place(1, t, part[0:8], part[8:16])
            meet_gather(step, 0, t)

    def local_faces(c, _):
        for number, face in enumerate(by_product):
            both = jnp.dot(heads[face ^ 1], chosen[number, c], preferred_element_type=jnp.float32)
            value = both[0:16] + both[16:32]
            for piece in range(WIDE // LANES):
                t = c * (WIDE // LANES) + piece
                part = value[:, piece * LANES : (piece + 1) * LANES]
                if face < 2:
                    met[face, t] = part
                else:
                    place(face, t, part[0:8], part[8:16])
        for face in by_gather:
            sources = [local_source(face ^ 1, s) for s in range(tiles)]
            for piece in range(WIDE // LANES):
                t = c * (WIDE // LANES) + piece
                upper, lower = pick(sources, wide_index(near_in, face, t))
                if face < 2:
                    met[face, t, 0:8, :] = upper
                    met[face, t, 8:16, :] = lower
                else:
                    place(face, t, upper, lower)
        return 0

    def outer_faces(step):
        def body(t, _):
            for face in range(2):
                meet_gather(step, face, t)
            return 0

        return body

    copies = send_halo(0)

    def spots(t, _):
        row = lax.broadcasted_iota(jnp.int32, (16, LANES), 0)
        at = pl.multiple_of(t * LANES, LANES)
        for face in range(6):
            code = jnp.broadcast_to(turn_in[face : face + 1, pl.ds(at, LANES)], (16, LANES))
            a, b = row >> 2, row & 3
            a = jnp.where((code & 1) != 0, 3 - a, a)
            b = jnp.where((code & 2) != 0, 3 - b, b)
            spot[face, t] = jnp.where((code & 4) != 0, 4 * b + a, 4 * a + b)
        return 0

    loads["turn"].wait()
    lax.fori_loop(0, tiles, spots, 0)
    for tile in range(tiles):
        keep_outer(tile)
        keep_inner(tile)

    def fine_matrix():
        loads["stiff"].wait()
        loads["lift"].wait()
        lifting = lift_in[...]
        row64 = lax.broadcasted_iota(jnp.int32, (64, 64), 0)
        col64 = lax.broadcasted_iota(jnp.int32, (64, 64), 1)
        unit = jnp.where(row64 == col64, 1.0, 0.0).astype(jnp.float32)
        joined[:, 0:64] = stiff_in[...] - exact(lifting, selection()) + unit
        joined[:, 64:160] = lifting
        keep_split(weights, joined[...])

    def coarse_matrices():
        loads["coarse"].wait()
        one = coarse_in[...]
        two = exact(one, one)
        three = exact(two, one)
        four = exact(two, two)
        keep_split(one_power, one)
        keep_split(last_power, four)
        for part in range(2):
            for at, power in enumerate((one, two, three)):
                value = parts_of(power)[part]
                powers[192 * part + 64 * at : 192 * part + 64 * at + 64, :] = value
        zero = jnp.zeros((64, 64), jnp.float32)
        table = ((one, zero, zero), (two, one, zero), (three, two, one))
        for i in range(3):
            line = jnp.concatenate(table[i], axis=1)
            head, tail = parts_of(line)
            reach[64 * i : 64 * i + 64, :] = head
            reach[192 + 64 * i : 256 + 64 * i, :] = tail

    def coarse_first():
        loads["start"].wait()
        for c in range(elements // WIDE):
            columns = start_in[0, :, c * WIDE : (c + 1) * WIDE]
            coarse_start[c] = jnp.where(me_t == 0, 0.0, split_dot(one_power, columns))

    def advance(c):
        operand = jnp.concatenate([stack[2 * c], stack[2 * c + 1]], axis=1)
        state = operand[0:64]
        rate = split_dot(weights, operand) - state * state * state
        return state + time_step * rate

    for step in range(STEPS):
        if step > 0:
            for tile in range(tiles):
                keep_outer(tile)
            copies = send_halo(step)
            for tile in range(tiles):
                keep_inner(tile)
        if step == 0:
            fine_matrix()
            loads["near"].wait()
            lax.fori_loop(0, tiles, choose, 0)
            if small:
                lax.fori_loop(0, bound_tiles, choose_met, 0)
                lax.fori_loop(0, tiles, choose_sent, 0)
        lax.fori_loop(0, elements // WIDE, local_faces, 0, unroll=4)
        if step == 1:
            coarse_matrices()
        if step == 2:
            coarse_first()
        for copy in copies:
            copy.wait()
        if small:
            parts = halo_parts(step, 1)
            for c in range(elements // WIDE):
                meet(step, c, parts)
        else:
            lax.fori_loop(0, tiles, outer_faces(step), 0, unroll=4)
        if step < STEPS - 1:
            for c in range(elements // WIDE):
                later = advance(c)
                stack[2 * c, 0:64, :] = later[:, :LANES]
                stack[2 * c + 1, 0:64, :] = later[:, LANES:]

    pairs = (None, rank + 1 - 2 * (rank % 2), (rank + 2) % GROUP, GROUP - 1 - rank)

    def swap(source, target, send, recv, by, half):
        other = pairs[by]
        return pltpu.make_async_remote_copy(
            src_ref=source.at[other, half],
            dst_ref=target.at[rank, half],
            send_sem=send.at[by - 1, half],
            recv_sem=recv.at[by - 1, half],
            device_id=(first + other, me_s),
            device_id_type=MESH,
        )

    def last_step(q, target, slot):
        for w in range(quarter // WIDE):
            c = q * (quarter // WIDE) + w
            value = advance(c) - coarse_start[c]
            for piece in range(2):
                at = w * WIDE + piece * LANES
                half, column = at // (quarter // 2), at % (quarter // 2)
                target[slot, half, :, column : column + LANES] = value[
                    :, piece * LANES : (piece + 1) * LANES
                ]

    mixes = {(by, h): swap(defect, gathered, mix_send, mix_recv, by, h) for by in (2, 3, 1) for h in (0, 1)}
    for by in (2, 3, 1):
        last_step(pairs[by], defect, pairs[by])
        mixes[by, 0].start()
    for by in (2, 3, 1):
        mixes[by, 1].start()
    last_step(rank, gathered, rank)

    chain = [
        pltpu.make_async_remote_copy(
            src_ref=ends.at[GROUP - 1, h],
            dst_ref=carry.at[h],
            send_sem=chain_send.at[h],
            recv_sem=chain_recv.at[h],
            device_id=(following, me_s),
            device_id_type=MESH,
        )
        for h in range(2)
    ]
    backs = {(by, h): swap(ends, final, back_send, back_recv, by, h) for by in (2, 3, 1) for h in (0, 1)}

    def give_back(h):
        for by in (2, 3, 1):
            backs[by, h].start()
        final[rank, h] = ends[rank, h]

    for h in range(2):
        for by in (1, 2, 3):
            mixes[by, h].wait_recv()
        inputs = jnp.concatenate([gathered[0, h], gathered[1, h], gathered[2, h]], axis=0)
        reached = split_dot(reach, inputs)
        ends[0, h] = gathered[0, h]
        for m in range(1, GROUP):
            ends[m, h] = gathered[m, h] + reached[64 * m - 64 : 64 * m]

        @pl.when(group == 0)
        def _():
            if groups > 1:
                chain[h].start()
            give_back(h)

    @pl.when(group > 0)
    def _():
        for h in range(2):
            chain[h].wait_recv()
            held = carry[h]
            ends[GROUP - 1, h] = ends[GROUP - 1, h] + split_dot(last_power, held)

            @pl.when(group < groups - 1)
            def _():
                chain[h].start()

            spread = split_dot(powers, held)
            for m in range(GROUP - 1):
                ends[m, h] = ends[m, h] + spread[64 * m : 64 * m + 64]
            give_back(h)

    for copy in mixes.values():
        copy.wait_send()

    @pl.when(group < groups - 1)
    def _():
        for h in range(2):
            chain[h].wait_send()

    for h in range(2):
        for by in (1, 2, 3):
            backs[by, h].wait()
        for q in range(GROUP):
            at = q * quarter + h * (quarter // 2)
            out_ref[0, :, at : at + quarter // 2] = final[q, h]


def shards(start_state, stiffness, lifting, coarse, neighbor, orientation, send_low, send_high):
    elements = start_state.shape[2]
    bound = send_low.shape[0]
    tiles, bound_tiles, quarter = elements // LANES, bound // LANES, elements // GROUP
    f32, b16, i32 = jnp.float32, jnp.bfloat16, jnp.int32
    dma = pltpu.SemaphoreType.DMA
    vmem = pl.BlockSpec(memory_space=pltpu.VMEM)
    return pl.pallas_call(
        functools.partial(kernel, lax.axis_size("tm"), lax.axis_size("space")),
        out_shape=jax.ShapeDtypeStruct(start_state.shape, f32),
        in_specs=[pl.BlockSpec(memory_space=pltpu.HBM)] * 8,
        out_specs=vmem,
        scratch_shapes=[
            pltpu.VMEM((tiles, 160, LANES), f32),
            pltpu.VMEM((tiles, 4, 16, LANES), f32),
            pltpu.VMEM((6, 32, elements), b16),
            pltpu.VMEM((4, elements // WIDE, elements, WIDE), b16),
            pltpu.VMEM((elements, bound) if elements <= 1024 else (16, LANES), b16),
            pltpu.VMEM((elements // WIDE, bound, WIDE) if elements <= 1024 else (1, 16, LANES), b16),
            pltpu.VMEM((2, tiles, 16, LANES), f32),
            pltpu.VMEM((6, tiles, 16, LANES), i32),
            pltpu.VMEM((elements // WIDE, 64, WIDE), f32),
            pltpu.VMEM((STEPS, 2, bound_tiles, 16, LANES), f32),
            pltpu.VMEM((STEPS, 2, bound_tiles, 16, LANES), f32),
            pltpu.VMEM((64, 160), f32),
            pltpu.VMEM((128, 160), b16),
            pltpu.VMEM((384, 192), b16),
            pltpu.VMEM((384, 64), b16),
            pltpu.VMEM((128, 64), b16),
            pltpu.VMEM((128, 64), b16),
            pltpu.VMEM((GROUP, 2, 64, quarter // 2), f32),
            pltpu.VMEM((GROUP, 2, 64, quarter // 2), f32),
            pltpu.VMEM((2, 64, quarter // 2), f32),
            pltpu.VMEM((GROUP, 2, 64, quarter // 2), f32),
            pltpu.VMEM((GROUP, 2, 64, quarter // 2), f32),
            pltpu.VMEM((1, 64, elements), f32),
            pltpu.VMEM((64, 64), f32),
            pltpu.VMEM((64, 96), f32),
            pltpu.VMEM((64, 64), f32),
            pltpu.VMEM((6, elements), i32),
            pltpu.VMEM((6, elements), i32),
            pltpu.VMEM((1, bound), i32),
            pltpu.VMEM((1, bound), i32),
            dma((8,)),
            dma((tiles,)),
            dma((STEPS, 2)),
            dma((STEPS, 2)),
            dma((GROUP - 1, 2)),
            dma((GROUP - 1, 2)),
            dma((2,)),
            dma((2,)),
            dma((GROUP - 1, 2)),
            dma((GROUP - 1, 2)),
        ],
        compiler_params=pltpu.CompilerParams(
            collective_id=0, has_side_effects=True, vmem_limit_bytes=63 * 1024 * 1024
        ),
    )(
        start_state, stiffness, lifting, coarse, neighbor, orientation,
        send_low.reshape(1, bound), send_high.reshape(1, bound),
    )


def solution(mesh):
    return jax.shard_map(
        shards,
        mesh=mesh,
        in_specs=(
            P("tm", None, "space"),
            P(),
            P(),
            P(),
            P(None, "space"),
            P(None, "space"),
            P("space"),
            P("space"),
        ),
        out_specs=P("tm", None, "space"),
        check_vma=False,
    )
```

```python
import functools

import jax
import jax.numpy as jnp
from jax import lax
from jax.experimental import pallas as pl
from jax.experimental.pallas import tpu as pltpu
from jax.sharding import PartitionSpec as P

STEPS = 3
GROUP = 4
LANES = 128
WIDE = 256
MESH = pl.DeviceIdType.MESH

time_step = 0.05


def exact(a, b):
    return jnp.dot(a, b, precision=lax.Precision.HIGHEST, preferred_element_type=jnp.float32)


def parts_of(value):
    head = value.astype(jnp.bfloat16)
    tail = (value - head.astype(jnp.float32)).astype(jnp.bfloat16)
    return head, tail


def keep_split(ref, value):
    rows = value.shape[0]
    head, tail = parts_of(value)
    ref[0:rows, :] = head
    ref[rows : 2 * rows, :] = tail


def split_dot(ref, value):
    rows = ref.shape[0] // 2
    head, tail = parts_of(value)
    both = jnp.dot(ref[...], head, preferred_element_type=jnp.float32)
    rest = jnp.dot(ref[0:rows, :], tail, preferred_element_type=jnp.float32)
    return both[:rows] + (both[rows:] + rest)


def along(value, index, axis):
    return jnp.take_along_axis(value, index, axis=axis, mode="promise_in_bounds")


def pick(sources, index, upper=None, lower=None):
    lane = index & (LANES - 1)
    tile = index >> 7
    for number, load in sources:
        first, second = load()
        first, second = along(first, lane, 1), along(second, lane, 1)
        if upper is None:
            upper, lower = first, second
        else:
            here = tile == number
            upper, lower = jnp.where(here, first, upper), jnp.where(here, second, lower)
    return upper, lower


def selection():
    row = lax.broadcasted_iota(jnp.int32, (96, 64), 0)
    node = lax.broadcasted_iota(jnp.int32, (96, 64), 1)
    face, a, b = row >> 4, (row >> 2) & 3, row & 3
    place = jnp.where(
        face < 2, 4 * a + b, jnp.where(face < 4, 16 * a + b, 16 * a + 4 * b)
    ) + jnp.where(face == 1, 48, jnp.where(face == 3, 12, jnp.where(face == 5, 3, 0)))
    return jnp.where(place == node, 1.0, 0.0).astype(jnp.float32)


def kernel(
    n_time, n_space,
    start_ref, stiff_ref, lift_ref, coarse_ref, near_ref, turn_ref, low_ref, high_ref,
    out_ref,
    stack, trace, heads, chosen, send_hot, meet_hot, met, spot, coarse_start, leave, halo, joined, weights, outer_weights, base, reach, powers, last_power, one_power,
    defect, gathered, carry, ends, final,
    start_in, stiff_in, lift_in, coarse_in, near_in, turn_in, low_in, high_in, load_sem, state_sem,
    halo_send, halo_recv, mix_send, mix_recv, chain_send, chain_recv, back_send, back_recv,
):
    elements = start_ref.shape[2]
    loads = {}
    for number, (name, source, target) in enumerate(
        (
            ("low", low_ref, low_in),
            ("high", high_ref, high_in),
            ("turn", turn_ref, turn_in),
            ("stiff", stiff_ref, stiff_in),
            ("lift", lift_ref, lift_in),
            ("near", near_ref, near_in),
            ("coarse", coarse_ref, coarse_in),
            ("start", start_ref, start_in),
        )
    ):
        loads[name] = pltpu.make_async_copy(source, target, load_sem.at[number])
    for name in ("low", "high"):
        loads[name].start()
    states = []
    for tile in range(elements // LANES):
        states.append(
            pltpu.make_async_copy(
                start_ref.at[0, :, tile * LANES : (tile + 1) * LANES],
                stack.at[tile, 0:64, :],
                state_sem.at[tile],
            )
        )
        states[-1].start()
    for name in ("turn", "stiff", "lift", "near", "coarse", "start"):
        loads[name].start()
    small = elements <= 1024
    by_product, by_gather = (1, 3, 4, 5), (0, 2)
    tiles = elements // LANES
    bound = low_ref.shape[1]
    bound_tiles = bound // LANES
    quarter = elements // GROUP
    me_t, me_s = lax.axis_index("tm"), lax.axis_index("space")
    group, rank = me_t // GROUP, me_t % GROUP
    first = group * GROUP
    groups = n_time // GROUP
    below, above = (me_s + n_space - 1) % n_space, (me_s + 1) % n_space
    mates = [first + (rank + by) % GROUP for by in range(1, GROUP)]
    following = (me_t + GROUP) % n_time
    previous = (me_t + n_time - GROUP) % n_time

    barrier = pltpu.get_barrier_semaphore()
    for space in (below, above):
        pl.semaphore_signal(barrier, inc=1, device_id=(me_t, space), device_id_type=MESH)
    for time in mates + [following, previous]:
        pl.semaphore_signal(barrier, inc=1, device_id=(time, me_s), device_id_type=MESH)

    def keep_parts(face, tile, value):
        head, tail = parts_of(value)
        heads[face, 0:16, tile * LANES : (tile + 1) * LANES] = head
        heads[face, 16:32, tile * LANES : (tile + 1) * LANES] = tail

    def keep_outer(tile):
        for face in range(2):
            keep_parts(face, tile, stack[tile, 48 * face : 48 * face + 16, :])

    def keep_inner(tile):
        for i in range(4):
            trace[tile, 0, 4 * i : 4 * i + 4, :] = stack[tile, 16 * i : 16 * i + 4, :]
            trace[tile, 1, 4 * i : 4 * i + 4, :] = stack[tile, 16 * i + 12 : 16 * i + 16, :]
        trace[tile, 2] = stack[tile, pl.ds(0, 16, stride=4), :]
        trace[tile, 3] = stack[tile, pl.ds(3, 16, stride=4), :]
        for face in range(2, 6):
            keep_parts(face, tile, trace[tile, face - 2])

    loads["low"].wait()
    loads["high"].wait()
    for copy in states:
        copy.wait()

    def local_source(face, s):
        if face == 0:
            return s, lambda: (stack[s, 0:8, :], stack[s, 8:16, :])
        if face == 1:
            return s, lambda: (stack[s, 48:56, :], stack[s, 56:64, :])
        return s, lambda: (trace[s, face - 2, 0:8, :], trace[s, face - 2, 8:16, :])

    def wide_index(ref, row, t):
        at = pl.multiple_of(t * LANES, LANES)
        return jnp.broadcast_to(ref[row : row + 1, pl.ds(at, LANES)], (8, LANES))

    def halo_copies(step):
        return [
            pltpu.make_async_remote_copy(
                src_ref=leave.at[step, side],
                dst_ref=halo.at[step, side],
                send_sem=halo_send.at[step, side],
                recv_sem=halo_recv.at[step, side],
                device_id=(me_t, target),
                device_id_type=MESH,
            )
            for side, target in ((0, below), (1, above))
        ]

    def send_halo(step):
        def fill(side, ref, t):
            sources = [local_source(side, s) for s in range(tiles)]
            upper, lower = pick(sources, wide_index(ref, 0, t))
            leave[step, side, t, 0:8, :] = upper
            leave[step, side, t, 8:16, :] = lower

        both_sides = step == 0 or not small
        if not both_sides:
            both = jnp.dot(heads[1], send_hot[...], preferred_element_type=jnp.float32)
            value = both[0:16] + both[16:32]
            for b in range(bound_tiles):
                leave[step, 1, b] = value[:, b * LANES : (b + 1) * LANES]
        for t in range(bound_tiles):
            fill(0, low_in, t)
            if both_sides:
                fill(1, high_in, t)
        if step == 0:
            pl.semaphore_wait(barrier, 2 + GROUP - 1 + 2)
        copies = halo_copies(step)
        for copy in copies:
            copy.start()
        return copies

    def place(face, t, upper, lower):
        for half in range(2):
            index = spot[face, t, 8 * half : 8 * half + 8, :]
            row = index & 7
            turned = jnp.where(index < 8, along(upper, row, 0), along(lower, row, 0))
            at = 64 + 16 * face + 8 * half
            stack[t, at : at + 8, :] = turned

    def one_hot(index, k):
        row = lax.broadcasted_iota(jnp.int32, (LANES, index.shape[1]), 0)
        row = row.astype(jnp.float32).astype(jnp.bfloat16)
        inside = jnp.clip(index - k * LANES, -1, LANES).astype(jnp.float32).astype(jnp.bfloat16)
        inside = jnp.broadcast_to(inside, row.shape)
        return jnp.where(row == inside, jnp.ones_like(row), jnp.zeros_like(row))

    def choose(k, _):
        at = pl.ds(pl.multiple_of(k * LANES, LANES), LANES)
        for number, face in enumerate(by_product):
            for c in range(elements // WIDE):
                index = near_in[face : face + 1, c * WIDE : (c + 1) * WIDE]
                chosen[number, c, at, :] = one_hot(index, k)
        return 0

    def choose_sent(k, _):
        at = pl.ds(pl.multiple_of(k * LANES, LANES), LANES)
        send_hot[at, :] = one_hot(high_in[...], k)
        return 0

    def choose_met(k, _):
        at = pl.ds(pl.multiple_of(k * LANES, LANES), LANES)
        for c in range(elements // WIDE):
            index = near_in[1:2, c * WIDE : (c + 1) * WIDE]
            meet_hot[c, at, :] = one_hot(index - (elements + bound), k)
        return 0

    def halo_parts(step, face):
        tiles_in = [halo[step, 1 - face, b] for b in range(bound_tiles)]
        head, tail = parts_of(jnp.concatenate(tiles_in, axis=1))
        return jnp.concatenate([head, tail], axis=0)

    def halo_sources(step, face):
        sources = []
        for b in range(bound_tiles):
            number = tiles + face * bound_tiles + b
            sources.append(
                (
                    number,
                    lambda b=b: (
                        halo[step, 1 - face, b, 0:8, :],
                        halo[step, 1 - face, b, 8:16, :],
                    ),
                )
            )
        return sources

    def meet_gather(step, face, t):
        inside = met[face, t, 0:8, :], met[face, t, 8:16, :]
        index = wide_index(near_in, face, t)
        place(face, t, *pick(halo_sources(step, face), index, *inside))

    def meet(step, c, parts):
        both = jnp.dot(parts, meet_hot[c], preferred_element_type=jnp.float32)
        value = both[0:16] + both[16:32]
        for piece in range(WIDE // LANES):
            t = c * (WIDE // LANES) + piece
            part = met[1, t] + value[:, piece * LANES : (piece + 1) * LANES]
            place(1, t, part[0:8], part[8:16])
            meet_gather(step, 0, t)

    def local_faces(c, _):
        for number, face in enumerate(by_product):
            both = jnp.dot(heads[face ^ 1], chosen[number, c], preferred_element_type=jnp.float32)
            value = both[0:16] + both[16:32]
            for piece in range(WIDE // LANES):
                t = c * (WIDE // LANES) + piece
                part = value[:, piece * LANES : (piece + 1) * LANES]
                if face < 2:
                    met[face, t] = part
                else:
                    place(face, t, part[0:8], part[8:16])
        for face in by_gather:
            sources = [local_source(face ^ 1, s) for s in range(tiles)]
            for piece in range(WIDE // LANES):
                t = c * (WIDE // LANES) + piece
                upper, lower = pick(sources, wide_index(near_in, face, t))
                if face < 2:
                    met[face, t, 0:8, :] = upper
                    met[face, t, 8:16, :] = lower
                else:
                    place(face, t, upper, lower)
        return 0

    def outer_faces(step):
        def body(t, _):
            for face in range(2):
                meet_gather(step, face, t)
            return 0

        return body

    copies = send_halo(0)

    def spots(t, _):
        row = lax.broadcasted_iota(jnp.int32, (16, LANES), 0)
        at = pl.multiple_of(t * LANES, LANES)
        for face in range(6):
            code = jnp.broadcast_to(turn_in[face : face + 1, pl.ds(at, LANES)], (16, LANES))
            a, b = row >> 2, row & 3
            a = jnp.where((code & 1) != 0, 3 - a, a)
            b = jnp.where((code & 2) != 0, 3 - b, b)
            spot[face, t] = jnp.where((code & 4) != 0, 4 * b + a, 4 * a + b)
        return 0

    loads["turn"].wait()
    lax.fori_loop(0, tiles, spots, 0)
    for tile in range(tiles):
        keep_outer(tile)
        keep_inner(tile)

    def fine_matrix():
        loads["stiff"].wait()
        loads["lift"].wait()
        lifting = lift_in[...]
        row64 = lax.broadcasted_iota(jnp.int32, (64, 64), 0)
        col64 = lax.broadcasted_iota(jnp.int32, (64, 64), 1)
        unit = jnp.where(row64 == col64, 1.0, 0.0).astype(jnp.float32)
        joined[:, 0:64] = stiff_in[...] - exact(lifting, selection()) + unit
        joined[:, 64:160] = lifting
        whole = joined[...]
        keep_split(weights, jnp.concatenate([whole[:, 0:64], whole[:, 96:160]], axis=1))
        keep_split(outer_weights, whole[:, 64:96])

    def coarse_matrices():
        one = coarse_in[...]
        two = exact(one, one)
        three = exact(two, one)
        four = exact(two, two)
        keep_split(last_power, four)
        for part in range(2):
            for at, power in enumerate((one, two, three)):
                value = parts_of(power)[part]
                powers[192 * part + 64 * at : 192 * part + 64 * at + 64, :] = value
        zero = jnp.zeros((64, 64), jnp.float32)
        table = ((one, zero, zero), (two, one, zero), (three, two, one))
        for i in range(3):
            line = jnp.concatenate(table[i], axis=1)
            head, tail = parts_of(line)
            reach[64 * i : 64 * i + 64, :] = head
            reach[192 + 64 * i : 256 + 64 * i, :] = tail

    def coarse_first():
        loads["start"].wait()
        loads["coarse"].wait()
        keep_split(one_power, coarse_in[...])
        for c in range(elements // WIDE):
            columns = start_in[0, :, c * WIDE : (c + 1) * WIDE]
            coarse_start[c] = jnp.where(me_t == 0, 0.0, split_dot(one_power, columns))

    def begin(c):
        operand = jnp.concatenate([stack[2 * c], stack[2 * c + 1]], axis=1)
        state = operand[0:64]
        known = jnp.concatenate([state, operand[96:160]], axis=0)
        base[c] = state + time_step * (split_dot(weights, known) - state * state * state)

    def advance(c):
        outer = jnp.concatenate([stack[2 * c, 64:96, :], stack[2 * c + 1, 64:96, :]], axis=1)
        return base[c] + time_step * split_dot(outer_weights, outer)

    for step in range(STEPS):
        if step > 0:
            for tile in range(tiles):
                keep_outer(tile)
            copies = send_halo(step)
            for tile in range(tiles):
                keep_inner(tile)
        if step == 0:
            fine_matrix()
            loads["near"].wait()
            lax.fori_loop(0, tiles, choose, 0)
            if small:
                lax.fori_loop(0, bound_tiles, choose_met, 0)
                lax.fori_loop(0, tiles, choose_sent, 0)
        lax.fori_loop(0, elements // WIDE, local_faces, 0, unroll=4)
        for c in range(elements // WIDE):
            begin(c)
        if step == 2:
            coarse_first()
        for copy in copies:
            copy.wait()
        if small:
            parts = halo_parts(step, 1)
            for c in range(elements // WIDE):
                meet(step, c, parts)
        else:
            lax.fori_loop(0, tiles, outer_faces(step), 0, unroll=4)
        if step < STEPS - 1:
            for c in range(elements // WIDE):
                later = advance(c)
                stack[2 * c, 0:64, :] = later[:, :LANES]
                stack[2 * c + 1, 0:64, :] = later[:, LANES:]

    pairs = (None, rank + 1 - 2 * (rank % 2), (rank + 2) % GROUP, GROUP - 1 - rank)

    def swap(source, target, send, recv, by, half):
        other = pairs[by]
        return pltpu.make_async_remote_copy(
            src_ref=source.at[other, half],
            dst_ref=target.at[rank, half],
            send_sem=send.at[by - 1, half],
            recv_sem=recv.at[by - 1, half],
            device_id=(first + other, me_s),
            device_id_type=MESH,
        )

    def last_step(q, target, slot):
        for w in range(quarter // WIDE):
            c = q * (quarter // WIDE) + w
            value = advance(c) - coarse_start[c]
            for piece in range(2):
                at = w * WIDE + piece * LANES
                half, column = at // (quarter // 2), at % (quarter // 2)
                target[slot, half, :, column : column + LANES] = value[
                    :, piece * LANES : (piece + 1) * LANES
                ]

    mixes = {(by, h): swap(defect, gathered, mix_send, mix_recv, by, h) for by in (2, 3, 1) for h in (0, 1)}
    for by in (2, 3, 1):
        last_step(pairs[by], defect, pairs[by])
        mixes[by, 0].start()
    for by in (2, 3, 1):
        mixes[by, 1].start()
    last_step(rank, gathered, rank)
    coarse_matrices()

    chain = [
        pltpu.make_async_remote_copy(
            src_ref=ends.at[GROUP - 1, h],
            dst_ref=carry.at[h],
            send_sem=chain_send.at[h],
            recv_sem=chain_recv.at[h],
            device_id=(following, me_s),
            device_id_type=MESH,
        )
        for h in range(2)
    ]
    backs = {(by, h): swap(ends, final, back_send, back_recv, by, h) for by in (2, 3, 1) for h in (0, 1)}

    def give_back(h):
        for by in (2, 3, 1):
            backs[by, h].start()
        final[rank, h] = ends[rank, h]

    for h in range(2):
        for by in (1, 2, 3):
            mixes[by, h].wait_recv()
        inputs = jnp.concatenate([gathered[0, h], gathered[1, h], gathered[2, h]], axis=0)
        reached = split_dot(reach, inputs)
        ends[0, h] = gathered[0, h]
        for m in range(1, GROUP):
            ends[m, h] = gathered[m, h] + reached[64 * m - 64 : 64 * m]

        @pl.when(group == 0)
        def _():
            if groups > 1:
                chain[h].start()
            give_back(h)

    @pl.when(group > 0)
    def _():
        for h in range(2):
            chain[h].wait_recv()
            held = carry[h]
            ends[GROUP - 1, h] = ends[GROUP - 1, h] + split_dot(last_power, held)

            @pl.when(group < groups - 1)
            def _():
                chain[h].start()

            spread = split_dot(powers, held)
            for m in range(GROUP - 1):
                ends[m, h] = ends[m, h] + spread[64 * m : 64 * m + 64]
            give_back(h)

    for copy in mixes.values():
        copy.wait_send()

    @pl.when(group < groups - 1)
    def _():
        for h in range(2):
            chain[h].wait_send()

    for h in range(2):
        for by in (1, 2, 3):
            backs[by, h].wait()
        for q in range(GROUP):
            at = q * quarter + h * (quarter // 2)
            out_ref[0, :, at : at + quarter // 2] = final[q, h]


def shards(start_state, stiffness, lifting, coarse, neighbor, orientation, send_low, send_high):
    elements = start_state.shape[2]
    bound = send_low.shape[0]
    tiles, bound_tiles, quarter = elements // LANES, bound // LANES, elements // GROUP
    f32, b16, i32 = jnp.float32, jnp.bfloat16, jnp.int32
    dma = pltpu.SemaphoreType.DMA
    vmem = pl.BlockSpec(memory_space=pltpu.VMEM)
    return pl.pallas_call(
        functools.partial(kernel, lax.axis_size("tm"), lax.axis_size("space")),
        out_shape=jax.ShapeDtypeStruct(start_state.shape, f32),
        in_specs=[pl.BlockSpec(memory_space=pltpu.HBM)] * 8,
        out_specs=vmem,
        scratch_shapes=[
            pltpu.VMEM((tiles, 160, LANES), f32),
            pltpu.VMEM((tiles, 4, 16, LANES), f32),
            pltpu.VMEM((6, 32, elements), b16),
            pltpu.VMEM((4, elements // WIDE, elements, WIDE), b16),
            pltpu.VMEM((elements, bound) if elements <= 1024 else (16, LANES), b16),
            pltpu.VMEM((elements // WIDE, bound, WIDE) if elements <= 1024 else (1, 16, LANES), b16),
            pltpu.VMEM((2, tiles, 16, LANES), f32),
            pltpu.VMEM((6, tiles, 16, LANES), i32),
            pltpu.VMEM((elements // WIDE, 64, WIDE), f32),
            pltpu.VMEM((STEPS, 2, bound_tiles, 16, LANES), f32),
            pltpu.VMEM((STEPS, 2, bound_tiles, 16, LANES), f32),
            pltpu.VMEM((64, 160), f32),
            pltpu.VMEM((128, 128), b16),
            pltpu.VMEM((128, 32), b16),
            pltpu.VMEM((elements // WIDE, 64, WIDE), f32),
            pltpu.VMEM((384, 192), b16),
            pltpu.VMEM((384, 64), b16),
            pltpu.VMEM((128, 64), b16),
            pltpu.VMEM((128, 64), b16),
            pltpu.VMEM((GROUP, 2, 64, quarter // 2), f32),
            pltpu.VMEM((GROUP, 2, 64, quarter // 2), f32),
            pltpu.VMEM((2, 64, quarter // 2), f32),
            pltpu.VMEM((GROUP, 2, 64, quarter // 2), f32),
            pltpu.VMEM((GROUP, 2, 64, quarter // 2), f32),
            pltpu.VMEM((1, 64, elements), f32),
            pltpu.VMEM((64, 64), f32),
            pltpu.VMEM((64, 96), f32),
            pltpu.VMEM((64, 64), f32),
            pltpu.VMEM((6, elements), i32),
            pltpu.VMEM((6, elements), i32),
            pltpu.VMEM((1, bound), i32),
            pltpu.VMEM((1, bound), i32),
            dma((8,)),
            dma((tiles,)),
            dma((STEPS, 2)),
            dma((STEPS, 2)),
            dma((GROUP - 1, 2)),
            dma((GROUP - 1, 2)),
            dma((2,)),
            dma((2,)),
            dma((GROUP - 1, 2)),
            dma((GROUP - 1, 2)),
        ],
        compiler_params=pltpu.CompilerParams(
            collective_id=0, has_side_effects=True, vmem_limit_bytes=63 * 1024 * 1024
        ),
    )(
        start_state, stiffness, lifting, coarse, neighbor, orientation,
        send_low.reshape(1, bound), send_high.reshape(1, bound),
    )


def solution(mesh):
    return jax.shard_map(
        shards,
        mesh=mesh,
        in_specs=(
            P("tm", None, "space"),
            P(),
            P(),
            P(),
            P(None, "space"),
            P(None, "space"),
            P("space"),
            P("space"),
        ),
        out_specs=P("tm", None, "space"),
        check_vma=False,
    )
```
